32 devices in a mesh: groups: 2 (over y), gx: 16 (over z, x, core).
Axes of the slice: x: 2, y: 2, z: 4, core: 2. Of those that a mesh axis runs over, the one named last changes fastest.
Arguments:
- temp0: float32 [32, 32, 1024], P(('groups', 'gx')), parts along dimension 0, may hold values from 0.3 to 1.6
- kappa: float32 [32, 32, 1024], P(('groups', 'gx')), parts along dimension 0, may hold values from 0.5 to 1.5
- act_step: int32 [32, 32, 1024], P(('groups', 'gx')), parts along dimension 0, may hold values from 0 to 4
- hface: float32 [32, 1024], P(('groups', 'gx')), parts along dimension 0, may hold values from 0.2 to 2
- codes: int32 [32, 1024], P(('groups', 'gx')), parts along dimension 0, may hold values from 0 to 2
- path: int32 [8, 32], P('groups'), parts along dimension 0, may hold values from 0 to 16383
- cotangent: float32 [32, 32, 1024], P(('groups', 'gx')), parts along dimension 0, may hold values from -6 to 6
Outputs:
- adjoint: float32 [32, 32, 1024], P(('groups', 'gx')), parts along dimension 0
- kappa_grad: float32 [32, 32, 1024], P(('groups', 'gx')), parts along dimension 0
- hface_grad: float32 [32, 1024], P(('groups', 'gx')), parts along dimension 0
The draws below stay inside these ranges and needn't reach their ends.
There are 2 independent parts, one for each index of `groups`. The reference program is written for one: setup_inputs(seed, part) draws one part's arguments, and reference() takes and returns one part's arrays. A program takes and returns all parts, laid end to end along the dimension named above; each array names one. Nothing has to cross between parts.
All inputs are finite; a program needn't handle non-finite values.
Results may differ from the reference program's by a relative error of at most 0.0003.
Values sent between devices are 32-bit elements; how exact they have to be, the bound alone decides.
No kernel may reach another device: no remote copies, remote signals or barrier semaphores. Data moves between devices by JAX's collectives and lax.ppermute only.
A program may use at most 64 MiB of HBM per device.

```python
import math
import jax
import jax.numpy as jnp
from jax import lax

NZ = 32
NY = 1024
STEPS = 4
SPOTS = 32
NX = 16


def plant(values, stream_key, smallest, largest):
    index_at = [jax.random.randint(jax.random.fold_in(stream_key, axis), (), 0, length) for axis, length in enumerate(values.shape)]
    main_axis = values.shape.index(max(values.shape))
    neighbour = index_at[:main_axis] + [(index_at[main_axis] + 1) % values.shape[main_axis]] + index_at[main_axis + 1:]
    return values.at[tuple(index_at)].set(smallest).at[tuple(neighbour)].set(largest)


def steps_of(key, extent, split, least, high):
    factor_of = 1.0
    for position, shards_of in split:
        heights = jax.random.uniform(jax.random.fold_in(jax.random.fold_in(key, 6), position), (shards_of,), jnp.float32, least / len(split), high / len(split))
        factor_of = factor_of * jnp.repeat(jnp.exp(heights), extent[position] // shards_of).reshape((-1,) + (1,) * (len(extent) - 1 - position))
    return factor_of


def gaussian(own_key, extent, scale, reach, cuts=(), dtype=jnp.bfloat16):
    loudness = steps_of(own_key, extent, cuts, -0.22, 0.18) if cuts else 1.0
    entries = jax.random.normal(own_key, extent, jnp.float32) * scale * loudness
    return jnp.minimum(jnp.maximum(entries, -reach), reach).astype(dtype)


def setup_inputs(seed: int = 0, part: int = 0) -> dict:
    arg_keys = jax.random.split(jax.random.key(seed), 8)
    part_keys = jax.random.split(jax.random.fold_in(arg_keys[7], part), 8)
    temp0 = jnp.clip(0.3 + 1.3 * jax.random.uniform(part_keys[0], (NX, NZ, NY), jnp.float32) ** steps_of(part_keys[0], (NX, NZ, NY), ((0, 16),), -0.2, 0.2), 0.3, 1.6)
    kappa = jnp.clip(jnp.exp(math.log(1.5) - 1.0986123 * jax.random.uniform(part_keys[1], (NX, NZ, NY), jnp.float32) ** steps_of(part_keys[1], (NX, NZ, NY), ((0, 16),), -0.2, 0.2)), 0.5, 1.5)
    act_step = plant(jax.random.randint(part_keys[2], (NX, NZ, NY), 0, STEPS + 1), jax.random.fold_in(part_keys[2], 1), 0, STEPS).astype(jnp.int32)
    hface = jnp.clip(jnp.exp(math.log(2.0) - 2.3025851 * jax.random.uniform(part_keys[3], (NX, NY), jnp.float32) ** steps_of(part_keys[3], (NX, NY), ((0, 16),), -0.2, 0.2)), 0.2, 2.0)
    codes = plant(jax.random.randint(part_keys[4], (NX, NY), 0, 3), jax.random.fold_in(part_keys[4], 1), 0, 2).astype(jnp.int32)
    path = plant(jax.random.randint(part_keys[5], (STEPS, SPOTS), 0, NX * NY), jax.random.fold_in(part_keys[5], 1), 0, (NX * NY) - 1).astype(jnp.int32)
    cotangent = gaussian(part_keys[6], (NX, NZ, NY), 1.0, 6.0, ((0, 16),), jnp.float32)
    return {"temp0": temp0, "kappa": kappa, "act_step": act_step, "hface": hface, "codes": codes, "path": path, "cotangent": cotangent}


LATENT = 1.5
MELT = 1.0
SPREAD = 0.15
DELTA = 0.05
EMISSION = 0.1
POWER = 8.0
AMBIENT = 0.2
SUBSTRATE = 0.5

def conductivity(temp, kappa, active):
    return kappa * (1.0 + 0.5 * temp) * (0.1 + 0.9 * active)

def capacity(temp):
    return 1.0 + LATENT * jnp.exp(-jnp.square((temp - MELT) / SPREAD))

def harmonic(first, second):
    total = first + second
    return 2.0 * first * second / jnp.where(total > 0, total, 1.0)

def heating(spots, offset, planes, cols):
    xs = offset + lax.broadcasted_iota(jnp.int32, (1, planes, cols), 1)
    ys = lax.broadcasted_iota(jnp.int32, (1, planes, cols), 2)
    cells = xs * cols + ys
    hits = (spots[:, None, None] == cells).astype(jnp.float32)
    return POWER * lax.optimization_barrier(jnp.sum(hits, axis=0))

def advance(temp_ext, keff_ext, hface, codes, heat):
    pads = ((0, 0), (1, 1), (1, 1))
    tpad = jnp.pad(temp_ext, pads)
    kpad = jnp.pad(keff_ext, pads)
    center = tpad[1:-1, 1:-1, 1:-1]
    kcen = kpad[1:-1, 1:-1, 1:-1]
    flux = jnp.zeros_like(center)
    slices = [(slice(2, None), slice(1, -1), slice(1, -1)), (slice(None, -2), slice(1, -1), slice(1, -1)), (slice(1, -1), slice(2, None), slice(1, -1)), (slice(1, -1), slice(None, -2), slice(1, -1)), (slice(1, -1), slice(1, -1), slice(2, None)), (slice(1, -1), slice(1, -1), slice(None, -2))]
    for place in slices:
        flux = flux + harmonic(kcen, kpad[place]) * (tpad[place] - center)
    top = center[:, 0, :]
    fourth = top * top * top * top
    loss = jnp.where(codes == 0, hface * (top - AMBIENT), jnp.where(codes == 1, EMISSION * hface * (fourth - AMBIENT ** 4), hface * (top - SUBSTRATE)))
    surface = heat - loss
    depth = lax.broadcasted_iota(jnp.int32, (1, center.shape[1], 1), 1)
    flux = flux + jnp.where(depth == 0, surface[:, None, :], 0.0)
    return center + DELTA * flux / capacity(center)

def reference(temp0, kappa, act_step, hface, codes, path, cotangent):

    def run(temp, kappa_in, hface_in):
        for step in range(STEPS):
            active = (act_step <= step).astype(jnp.float32)
            keff = conductivity(temp, kappa_in, active)
            pads = ((1, 1), (0, 0), (0, 0))
            heat = heating(path[step], 0, NX, NY)
            temp = advance(jnp.pad(temp, pads), jnp.pad(keff, pads), hface_in, codes, heat)
        return temp
    final, pull = jax.vjp(run, temp0, kappa, hface)
    adjoint, kappa_grad, hface_grad = pull(cotangent)
    return (adjoint, kappa_grad, hface_grad)
```

```python
import math

import jax
import jax.numpy as jnp
from jax import lax
from jax.experimental import pallas as pl
from jax.experimental.pallas import tpu as pltpu
from jax.sharding import PartitionSpec as P

LATENT = 1.5
MELT = 1.0
SPREAD = 0.15
DELTA = 0.05
EMISSION = 0.1
POWER = 8.0
AMBIENT = 0.2
SUBSTRATE = 0.5

LANES = 128
HALF = 64
LEFT = 96
IN_ROWS = 88
OUT_ROWS = 40


def lane_iota(rows):
    return lax.broadcasted_iota(jnp.int32, (rows, LANES), 1)


def pack_kernel(parts, width, temp, kappa, act, hface, codes, cot, out):
    tiles = temp.shape[-1] // LANES

    def window(ref, start, rows):
        tile, off = divmod(start, LANES)

        def part(t):
            t = min(max(t, 0), tiles - 1)
            value = ref[0, :, t * LANES : (t + 1) * LANES] if len(ref.shape) == 3 else ref[:, t * LANES : (t + 1) * LANES]
            value = value.astype(jnp.float32)
            return value if off == 0 else pltpu.roll(value, LANES - off, axis=1)

        lane = lane_iota(rows)
        result = part(tile)
        if off > LANES - HALF - 7:
            result = jnp.where((lane >= LANES - off) & (lane < LEFT), part(tile + 1), result)
        if off < 7:
            result = jnp.where((lane >= LEFT) & (lane < LANES - off), part(tile - 1), result)
        return result

    rows = temp.shape[1]
    half = rows // 2
    lane = lane_iota(rows)
    for d in range(parts):
        start = d * width
        t = window(temp, start, rows)
        k = window(kappa, start, rows)
        a = window(act, start, rows)
        c = window(cot, start, rows)
        extra = jnp.where(
            lane >= 89,
            pltpu.roll(a, 96, axis=1),
            jnp.where(lane >= 75, pltpu.roll(c, 11, axis=1), pltpu.roll(c, 75, axis=1)),
        )
        out[d, 0:rows] = jnp.where((lane >= 71) & (lane < 121), extra, t)
        out[d, rows : 2 * rows] = jnp.where((lane >= 75) & (lane < 121), pltpu.roll(a, 50, axis=1), k)
        out[d, 2 * rows : 2 * rows + half] = jnp.where(
            lane[:half] < HALF, c[:half], pltpu.roll(c[half:], HALF, axis=1)
        )
        h = window(hface, start, 1)
        s = window(codes, start, 1)
        row = lax.broadcasted_iota(jnp.int32, (8, LANES), 0)
        out[d, 2 * rows + half : 2 * rows + half + 8] = jnp.where(row == 0, h, s)


def reciprocal(value):
    return 1.0 / value


def shares(first, second):
    total = first + second
    positive = total > 0
    inverse = reciprocal(jnp.where(positive, total, 1.0))
    return first * inverse, second * inverse, positive


def window_kernel(cols, width, path, got, out, temps, keffs, rates, gains, kap, acts, lam, mu, kgrad, heat, hcoef, hgrad):
    planes = got.shape[0]
    rows = temps.shape[2]
    half = rows // 2
    steps = path.shape[0]
    spots = path.shape[1]
    base = lax.axis_index("gx") * width
    lane = lane_iota(rows)
    depth = lax.broadcasted_iota(jnp.int32, (rows, LANES), 0)
    inner = depth < rows - 1
    top_row = lax.broadcasted_iota(jnp.int32, (8, LANES), 0) == 0

    lane_p = lane_iota(planes)
    col = base + jnp.where(lane_p < LEFT, lane_p, lane_p - LANES)
    cell = lax.broadcasted_iota(jnp.int32, (planes, LANES), 0) * cols + col
    cell = jnp.where((col >= 0) & (col < cols), cell, -1)
    for n in range(steps):
        count = jnp.zeros((planes, LANES), jnp.float32)
        for s in range(spots):
            count = count + jnp.where(cell == path[n, s], 1.0, 0.0)
        heat[n] = POWER * count

    column = base + jnp.where(lane < LEFT, lane, lane - LANES)
    inside = (column >= 0) & (column < cols)

    def active(act, n):
        return jnp.where(act <= n, 1.0, 0.1)

    def unpack(p, carry):
        a = got[p, 0:rows]
        b = got[p, rows : 2 * rows]
        c = got[p, 2 * rows : 2 * rows + half]
        temps[0, p] = a
        k = jnp.where(inside, b, 0.0)
        kap[p] = k
        act = jnp.where((lane < 25) | (lane >= 121), pltpu.roll(a, LANES - 96, axis=1), pltpu.roll(b, LANES - 50, axis=1))
        acts[p] = act
        cot = jnp.concatenate([c, pltpu.roll(c, HALF, axis=1)], axis=0)
        cot = jnp.where(
            lane < HALF,
            cot,
            jnp.where(lane < LEFT, pltpu.roll(a, LANES - 11, axis=1), pltpu.roll(a, LANES - 75, axis=1)),
        )
        lam[p] = cot
        keffs[0, p] = k * active(act, 0.0) * (1.0 + 0.5 * a)
        return carry

    lax.fori_loop(0, planes, unpack, 0)
    zero = jnp.zeros((rows, LANES), jnp.float32)
    for n in range(steps):
        temps[n, planes] = zero
        keffs[n, planes] = zero
    mu[planes] = zero

    def forward(n):
        def step(p, behind):
            t = temps[n, p]
            a = keffs[n, p]

            def flow(b, dt):
                total = a + b
                return a * b * reciprocal(jnp.where(total > 0, total, 1.0)) * dt

            fx = flow(keffs[n, p + 1], temps[n, p + 1] - t)
            fy = flow(pltpu.roll(a, LANES - 1, axis=1), pltpu.roll(t, LANES - 1, axis=1) - t)
            fz = flow(pltpu.roll(a, rows - 1, axis=0), jnp.where(inner, pltpu.roll(t, rows - 1, axis=0) - t, 0.0))
            flux = 2.0 * ((fx - behind) + (fy - pltpu.roll(fy, 1, axis=1)) + (fz - pltpu.roll(fz, 1, axis=0)))
            shifted = t - MELT
            bump = LATENT * jnp.exp2(jnp.square(shifted) * (-1.0 / (SPREAD * SPREAD * math.log(2.0))))
            inv_c = reciprocal(1.0 + bump)
            rate = DELTA * inv_c
            t8 = t[0:8]
            h = got[p, 2 * rows + half : 2 * rows + half + 1]
            code = got[p, 2 * rows + half + 1 : 2 * rows + half + 2]
            square = t8 * t8
            radiative = code == 1.0
            linear = t8 - jnp.where(code == 0.0, AMBIENT, SUBSTRATE)
            shape = jnp.where(radiative, EMISSION * (square * square - AMBIENT**4), linear)
            slope = jnp.where(radiative, 4.0 * EMISSION * square * t8, 1.0)
            surface = jnp.where(top_row, heat[n, pl.ds(p, 1)] - h * shape, 0.0)
            flux = jnp.concatenate([flux[0:8] + surface, flux[8:]], axis=0)
            dt = flux * rate
            gain = 1.0 + dt * (bump * inv_c) * (shifted * (2.0 / (SPREAD * SPREAD)))
            gain = jnp.concatenate([gain[0:8] - jnp.where(top_row, rate[0:8] * h * slope, 0.0), gain[8:]], axis=0)
            gains[n, p] = gain
            hcoef[n, pl.ds(p, 1)] = -(rate[0:8] * shape)[0:1]
            if n < steps - 1:
                rates[n, p] = rate
                after = t + dt
                temps[n + 1, p] = after
                keffs[n + 1, p] = kap[p] * active(acts[p], float(n + 1)) * (1.0 + 0.5 * after)
            else:
                mu[p] = lam[p] * rate
            return fx

        lax.fori_loop(0, planes, step, zero)

    for n in range(steps):
        forward(n)

    def backward(n):
        def step(p, carry):
            behind_e, behind_p = carry
            t = temps[n, p]
            a = keffs[n, p]
            m = mu[p]

            def adjoint(b, dt, dm):
                ra, rb, positive = shares(a, b)
                q = dt * dm
                energy = a * rb * dm
                return energy, rb * jnp.where(positive, rb, 1.0) * q, ra * jnp.where(positive, ra, 1.0) * q

            ex, px, qx = adjoint(keffs[n, p + 1], temps[n, p + 1] - t, mu[p + 1] - m)
            ey, py, qy = adjoint(
                pltpu.roll(a, LANES - 1, axis=1), pltpu.roll(t, LANES - 1, axis=1) - t, pltpu.roll(m, LANES - 1, axis=1) - m
            )
            ez, pz, qz = adjoint(
                pltpu.roll(a, rows - 1, axis=0),
                pltpu.roll(t, rows - 1, axis=0) - t,
                jnp.where(inner, pltpu.roll(m, rows - 1, axis=0) - m, 0.0),
            )
            energy = (ex - behind_e) + (ey - pltpu.roll(ey, 1, axis=1)) + (ez - pltpu.roll(ez, 1, axis=0))
            pull = (px + behind_p) + (py + pltpu.roll(qy, 1, axis=1)) + (pz + pltpu.roll(qz, 1, axis=0))
            on = active(acts[p], float(n))
            old = lam[p]
            new = old * gains[n, p] + 2.0 * energy - pull * (kap[p] * on)
            grad = pull * (on * (2.0 + t))
            hg = old[0:1] * hcoef[n, pl.ds(p, 1)]
            if n < steps - 1:
                grad = kgrad[p] + grad
                hg = hgrad[pl.ds(p, 1)] + hg
            if n > 0:
                lam[p] = new
                mu[p] = new * rates[n - 1, p]
                kgrad[p] = grad
                hgrad[pl.ds(p, 1)] = hg
            else:
                out[p, 0:rows] = jnp.where(lane < HALF, new, pltpu.roll(-grad, HALF, axis=1))
                out[p, rows : rows + 8] = jnp.broadcast_to(hg, (8, LANES))
            return ex, qx

        lax.fori_loop(0, planes, step, (zero, zero))

    for n in reversed(range(steps)):
        backward(n)


def unpack_kernel(width, got, adjoint, kgrad, hgrad):
    rows = adjoint.shape[1]
    per_tile = LANES // width
    lane = lane_iota(rows)
    for tile in range(adjoint.shape[2] // LANES):
        adj = grad = face = None
        for i in range(per_tile):
            part = got[tile * per_tile + i, 0:rows]
            other = pltpu.roll(part, (i * width + HALF) % LANES, axis=1)
            hface = got[tile * per_tile + i, rows : rows + 1]
            if i:
                part = pltpu.roll(part, i * width, axis=1)
                hface = pltpu.roll(hface, i * width, axis=1)
                adj = jnp.where(lane < i * width, adj, part)
                grad = jnp.where(lane < i * width, grad, other)
                face = jnp.where(lane[0:1] < i * width, face, hface)
            else:
                adj, grad, face = part, other, hface
        place = slice(tile * LANES, (tile + 1) * LANES)
        adjoint[0, :, place] = adj
        kgrad[0, :, place] = grad
        hgrad[:, place] = face


def body(temp0, kappa, act_step, hface, codes, path, cotangent):
    parts = lax.axis_size("gx")
    cols = temp0.shape[2]
    rows = temp0.shape[1]
    width = cols // parts
    planes = parts * temp0.shape[0]
    steps = path.shape[0]
    vmem = pl.BlockSpec(memory_space=pltpu.VMEM)
    smem = pl.BlockSpec(memory_space=pltpu.SMEM)
    params = pltpu.CompilerParams(vmem_limit_bytes=56 * 1024 * 1024)

    def pack(*refs):
        pack_kernel(parts, width, *refs)

    packed = pl.pallas_call(
        pack,
        out_shape=jax.ShapeDtypeStruct((parts, IN_ROWS, LANES), jnp.float32),
        in_specs=[vmem] * 6,
        out_specs=vmem,
        compiler_params=params,
    )(temp0, kappa, act_step, hface, codes, cotangent)
    got = lax.all_to_all(packed, "gx", 0, 0, tiled=True)

    def compute(*refs):
        window_kernel(cols, width, *refs)

    cube = (rows, LANES)
    result = pl.pallas_call(
        compute,
        out_shape=jax.ShapeDtypeStruct((planes, OUT_ROWS, LANES), jnp.float32),
        in_specs=[smem, vmem],
        out_specs=vmem,
        scratch_shapes=[
            pltpu.VMEM((steps, planes + 1) + cube, jnp.float32),
            pltpu.VMEM((steps, planes + 1) + cube, jnp.float32),
            pltpu.VMEM((steps - 1, planes) + cube, jnp.float32),
            pltpu.VMEM((steps, planes) + cube, jnp.float32),
            pltpu.VMEM((planes,) + cube, jnp.float32),
            pltpu.VMEM((planes,) + cube, jnp.float32),
            pltpu.VMEM((planes,) + cube, jnp.float32),
            pltpu.VMEM((planes + 1,) + cube, jnp.float32),
            pltpu.VMEM((planes,) + cube, jnp.float32),
            pltpu.VMEM((steps, planes, LANES), jnp.float32),
            pltpu.VMEM((steps, planes, LANES), jnp.float32),
            pltpu.VMEM((planes, LANES), jnp.float32),
        ],
        compiler_params=params,
    )(path, got)
    back = lax.all_to_all(result, "gx", 0, 0, tiled=True)

    def unpack(*refs):
        unpack_kernel(width, *refs)

    return pl.pallas_call(
        unpack,
        out_shape=(
            jax.ShapeDtypeStruct(temp0.shape, jnp.float32),
            jax.ShapeDtypeStruct(kappa.shape, jnp.float32),
            jax.ShapeDtypeStruct(hface.shape, jnp.float32),
        ),
        in_specs=[vmem],
        out_specs=(vmem, vmem, vmem),
        compiler_params=params,
    )(back)


def solution(mesh):
    placed = (
        P(("groups", "gx"), None, None),
        P(("groups", "gx"), None, None),
        P(("groups", "gx"), None, None),
        P(("groups", "gx"), None),
        P(("groups", "gx"), None),
        P("groups", None),
        P(("groups", "gx"), None, None),
    )
    return jax.shard_map(
        body,
        mesh=mesh,
        in_specs=placed,
        out_specs=(
            P(("groups", "gx"), None, None),
            P(("groups", "gx"), None, None),
            P(("groups", "gx"), None),
        ),
        check_vma=False,
    )
```

```python
import math

import jax
import jax.numpy as jnp
from jax import lax
from jax.experimental import pallas as pl
from jax.experimental.pallas import tpu as pltpu
from jax.sharding import PartitionSpec as P

LATENT = 1.5
MELT = 1.0
SPREAD = 0.15
DELTA = 0.05
EMISSION = 0.1
POWER = 8.0
AMBIENT = 0.2
SUBSTRATE = 0.5

LANES = 128
HALF = 64
LEFT = 96
IN_ROWS = 88
OUT_ROWS = 40
UNROLL = 8
MIB = 1024 * 1024


def lane_iota(rows):
    return lax.broadcasted_iota(jnp.int32, (rows, LANES), 1)


def pack_kernel(parts, width, *refs):
    sources, out, (temp, kappa, act, hface, codes, cot), done = refs[:6], refs[6], refs[7:13], refs[13]
    copies = [
        pltpu.make_async_copy(source, held, done.at[i])
        for i, (source, held) in enumerate(zip(sources, (temp, kappa, act, hface, codes, cot)))
    ]
    for copy in copies:
        copy.start()
    for copy in copies:
        copy.wait()
    tiles = temp.shape[-1] // LANES

    def window(ref, start, rows):
        tile, off = divmod(start, LANES)

        def part(t):
            t = min(max(t, 0), tiles - 1)
            value = ref[0, :, t * LANES : (t + 1) * LANES] if len(ref.shape) == 3 else ref[:, t * LANES : (t + 1) * LANES]
            value = value.astype(jnp.float32)
            return value if off == 0 else pltpu.roll(value, LANES - off, axis=1)

        lane = lane_iota(rows)
        result = part(tile)
        if off > LANES - HALF - 7:
            result = jnp.where((lane >= LANES - off) & (lane < LEFT), part(tile + 1), result)
        if off < 7:
            result = jnp.where((lane >= LEFT) & (lane < LANES - off), part(tile - 1), result)
        return result

    rows = temp.shape[1]
    half = rows // 2
    lane = lane_iota(rows)
    for d in range(parts):
        start = d * width
        t = window(temp, start, rows)
        k = window(kappa, start, rows)
        a = window(act, start, rows)
        c = window(cot, start, rows)
        extra = jnp.where(
            lane >= 89,
            pltpu.roll(a, 96, axis=1),
            jnp.where(lane >= 75, pltpu.roll(c, 11, axis=1), pltpu.roll(c, 75, axis=1)),
        )
        out[d, 0:rows] = jnp.where((lane >= 71) & (lane < 121), extra, t)
        out[d, rows : 2 * rows] = jnp.where((lane >= 75) & (lane < 121), pltpu.roll(a, 50, axis=1), k)
        out[d, 2 * rows : 2 * rows + half] = jnp.where(
            lane[:half] < HALF, c[:half], pltpu.roll(c[half:], HALF, axis=1)
        )
        h = window(hface, start, 1)
        s = window(codes, start, 1)
        row = lax.broadcasted_iota(jnp.int32, (8, LANES), 0)
        out[d, 2 * rows + half : 2 * rows + half + 8] = jnp.where(row == 0, h, s)


def reciprocal(value):
    return 1.0 / value


def shares(first, second):
    total = first + second
    positive = total > 0
    inverse = reciprocal(jnp.where(positive, total, 1.0))
    return first * inverse, second * inverse, positive


def window_kernel(cols, width, path, got, out, temps, keffs, rates, gains, kap, acts, lam, mu, kgrad, heat, hcoef, hgrad):
    planes = got.shape[0]
    rows = temps.shape[2]
    half = rows // 2
    steps = path.shape[0]
    spots = path.shape[1]
    base = lax.axis_index("gx") * width
    lane = lane_iota(rows)
    depth = lax.broadcasted_iota(jnp.int32, (rows, LANES), 0)
    inner = depth < rows - 1
    top_row = lax.broadcasted_iota(jnp.int32, (8, LANES), 0) == 0

    lane_p = lane_iota(planes)
    col = base + jnp.where(lane_p < LEFT, lane_p, lane_p - LANES)
    cell = lax.broadcasted_iota(jnp.int32, (planes, LANES), 0) * cols + col
    cell = jnp.where((col >= 0) & (col < cols), cell, -1)
    for n in range(steps):
        count = jnp.zeros((planes, LANES), jnp.float32)
        for s in range(spots):
            count = count + jnp.where(cell == path[n, s], 1.0, 0.0)
        heat[n] = POWER * count

    column = base + jnp.where(lane < LEFT, lane, lane - LANES)
    inside = (column >= 0) & (column < cols)

    def active(act, n):
        return jnp.where(act <= n, 1.0, 0.1)

    def unpack(p, carry):
        a = got[p, 0:rows]
        b = got[p, rows : 2 * rows]
        c = got[p, 2 * rows : 2 * rows + half]
        temps[0, p] = a
        k = jnp.where(inside, b, 0.0)
        kap[p] = k
        act = jnp.where((lane < 25) | (lane >= 121), pltpu.roll(a, LANES - 96, axis=1), pltpu.roll(b, LANES - 50, axis=1))
        acts[p] = act
        cot = jnp.concatenate([c, pltpu.roll(c, HALF, axis=1)], axis=0)
        cot = jnp.where(
            lane < HALF,
            cot,
            jnp.where(lane < LEFT, pltpu.roll(a, LANES - 11, axis=1), pltpu.roll(a, LANES - 75, axis=1)),
        )
        lam[p] = cot
        keffs[0, p] = k * active(act, 0.0) * (1.0 + 0.5 * a)
        return carry

    lax.fori_loop(0, planes, unpack, 0, unroll=UNROLL)
    zero = jnp.zeros((rows, LANES), jnp.float32)
    for n in range(steps):
        temps[n, planes] = zero
        keffs[n, planes] = zero
    mu[planes] = zero

    def forward(n):
        def step(p, behind):
            t = temps[n, p]
            a = keffs[n, p]

            def flow(b, dt):
                total = a + b
                return a * b * reciprocal(jnp.where(total > 0, total, 1.0)) * dt

            fx = flow(keffs[n, p + 1], temps[n, p + 1] - t)
            fy = flow(pltpu.roll(a, LANES - 1, axis=1), pltpu.roll(t, LANES - 1, axis=1) - t)
            fz = flow(pltpu.roll(a, rows - 1, axis=0), jnp.where(inner, pltpu.roll(t, rows - 1, axis=0) - t, 0.0))
            flux = 2.0 * ((fx - behind) + (fy - pltpu.roll(fy, 1, axis=1)) + (fz - pltpu.roll(fz, 1, axis=0)))
            shifted = t - MELT
            bump = LATENT * jnp.exp2(jnp.square(shifted) * (-1.0 / (SPREAD * SPREAD * math.log(2.0))))
            inv_c = reciprocal(1.0 + bump)
            rate = DELTA * inv_c
            t8 = t[0:8]
            h = got[p, 2 * rows + half : 2 * rows + half + 1]
            code = got[p, 2 * rows + half + 1 : 2 * rows + half + 2]
            square = t8 * t8
            radiative = code == 1.0
            linear = t8 - jnp.where(code == 0.0, AMBIENT, SUBSTRATE)
            shape = jnp.where(radiative, EMISSION * (square * square - AMBIENT**4), linear)
            slope = jnp.where(radiative, 4.0 * EMISSION * square * t8, 1.0)
            surface = jnp.where(top_row, heat[n, pl.ds(p, 1)] - h * shape, 0.0)
            flux = jnp.concatenate([flux[0:8] + surface, flux[8:]], axis=0)
            dt = flux * rate
            gain = 1.0 + dt * (bump * inv_c) * (shifted * (2.0 / (SPREAD * SPREAD)))
            gain = jnp.concatenate([gain[0:8] - jnp.where(top_row, rate[0:8] * h * slope, 0.0), gain[8:]], axis=0)
            gains[n, p] = gain
            hcoef[n, pl.ds(p, 1)] = -(rate[0:8] * shape)[0:1]
            if n < steps - 1:
                rates[n, p] = rate
                after = t + dt
                temps[n + 1, p] = after
                keffs[n + 1, p] = kap[p] * active(acts[p], float(n + 1)) * (1.0 + 0.5 * after)
            else:
                mu[p] = lam[p] * rate
            return fx

        lax.fori_loop(0, planes, step, zero, unroll=UNROLL)

    for n in range(steps):
        forward(n)

    def backward(n):
        def step(p, carry):
            behind_e, behind_p = carry
            t = temps[n, p]
            a = keffs[n, p]
            m = mu[p]

            def adjoint(b, dt, dm):
                ra, rb, positive = shares(a, b)
                q = dt * dm
                energy = a * rb * dm
                return energy, rb * jnp.where(positive, rb, 1.0) * q, ra * jnp.where(positive, ra, 1.0) * q

            ex, px, qx = adjoint(keffs[n, p + 1], temps[n, p + 1] - t, mu[p + 1] - m)
            ey, py, qy = adjoint(
                pltpu.roll(a, LANES - 1, axis=1), pltpu.roll(t, LANES - 1, axis=1) - t, pltpu.roll(m, LANES - 1, axis=1) - m
            )
            ez, pz, qz = adjoint(
                pltpu.roll(a, rows - 1, axis=0),
                pltpu.roll(t, rows - 1, axis=0) - t,
                jnp.where(inner, pltpu.roll(m, rows - 1, axis=0) - m, 0.0),
            )
            energy = (ex - behind_e) + (ey - pltpu.roll(ey, 1, axis=1)) + (ez - pltpu.roll(ez, 1, axis=0))
            pull = (px + behind_p) + (py + pltpu.roll(qy, 1, axis=1)) + (pz + pltpu.roll(qz, 1, axis=0))
            on = active(acts[p], float(n))
            old = lam[p]
            new = old * gains[n, p] + 2.0 * energy - pull * (kap[p] * on)
            grad = pull * (on * (2.0 + t))
            hg = old[0:1] * hcoef[n, pl.ds(p, 1)]
            if n < steps - 1:
                grad = kgrad[p] + grad
                hg = hgrad[pl.ds(p, 1)] + hg
            if n > 0:
                lam[p] = new
                mu[p] = new * rates[n - 1, p]
                kgrad[p] = grad
                hgrad[pl.ds(p, 1)] = hg
            else:
                out[p, 0:rows] = jnp.where(lane < HALF, new, pltpu.roll(-grad, HALF, axis=1))
                out[p, rows : rows + 8] = jnp.broadcast_to(hg, (8, LANES))
            return ex, qx

        lax.fori_loop(0, planes, step, (zero, zero), unroll=UNROLL)

    for n in reversed(range(steps)):
        backward(n)


def unpack_kernel(width, got, adjoint, kgrad, hgrad):
    rows = adjoint.shape[1]
    per_tile = LANES // width
    lane = lane_iota(rows)
    for tile in range(adjoint.shape[2] // LANES):
        adj = grad = face = None
        for i in range(per_tile):
            part = got[tile * per_tile + i, 0:rows]
            other = pltpu.roll(part, (i * width + HALF) % LANES, axis=1)
            hface = got[tile * per_tile + i, rows : rows + 1]
            if i:
                part = pltpu.roll(part, i * width, axis=1)
                hface = pltpu.roll(hface, i * width, axis=1)
                adj = jnp.where(lane < i * width, adj, part)
                grad = jnp.where(lane < i * width, grad, other)
                face = jnp.where(lane[0:1] < i * width, face, hface)
            else:
                adj, grad, face = part, other, hface
        place = slice(tile * LANES, (tile + 1) * LANES)
        adjoint[0, :, place] = adj
        kgrad[0, :, place] = grad
        hgrad[:, place] = face


def body(temp0, kappa, act_step, hface, codes, path, cotangent):
    parts = lax.axis_size("gx")
    cols = temp0.shape[2]
    rows = temp0.shape[1]
    width = cols // parts
    planes = parts * temp0.shape[0]
    steps = path.shape[0]
    vmem = pl.BlockSpec(memory_space=pltpu.VMEM)
    smem = pl.BlockSpec(memory_space=pltpu.SMEM)

    def params(words):
        return pltpu.CompilerParams(vmem_limit_bytes=4 * words + 2 * MIB)

    plane = rows * LANES

    def pack(*refs):
        pack_kernel(parts, width, *refs)

    packed = pl.pallas_call(
        pack,
        out_shape=jax.ShapeDtypeStruct((parts, IN_ROWS, LANES), jnp.float32),
        in_specs=[pl.BlockSpec(memory_space=pltpu.HBM)] * 6,
        out_specs=vmem,
        scratch_shapes=[pltpu.VMEM(x.shape, x.dtype) for x in (temp0, kappa, act_step, hface, codes, cotangent)]
        + [pltpu.SemaphoreType.DMA((6,))],
        compiler_params=params(4 * rows * cols + parts * IN_ROWS * LANES),
    )(*[pltpu.with_memory_space_constraint(x, pltpu.HBM) for x in (temp0, kappa, act_step, hface, codes, cotangent)])
    got = lax.all_to_all(packed, "gx", 0, 0, tiled=True)

    def compute(*refs):
        window_kernel(cols, width, *refs)

    cube = (rows, LANES)
    result = pl.pallas_call(
        compute,
        out_shape=jax.ShapeDtypeStruct((planes, OUT_ROWS, LANES), jnp.float32),
        in_specs=[smem, vmem],
        out_specs=vmem,
        scratch_shapes=[
            pltpu.VMEM((steps, planes + 1) + cube, jnp.float32),
            pltpu.VMEM((steps, planes + 1) + cube, jnp.float32),
            pltpu.VMEM((steps - 1, planes) + cube, jnp.float32),
            pltpu.VMEM((steps, planes) + cube, jnp.float32),
            pltpu.VMEM((planes,) + cube, jnp.float32),
            pltpu.VMEM((planes,) + cube, jnp.float32),
            pltpu.VMEM((planes,) + cube, jnp.float32),
            pltpu.VMEM((planes + 1,) + cube, jnp.float32),
            pltpu.VMEM((planes,) + cube, jnp.float32),
            pltpu.VMEM((steps, planes, LANES), jnp.float32),
            pltpu.VMEM((steps, planes, LANES), jnp.float32),
            pltpu.VMEM((planes, LANES), jnp.float32),
        ],
        compiler_params=params(planes * (24 * plane + (IN_ROWS + OUT_ROWS) * LANES)),
    )(path, got)
    back = lax.all_to_all(result, "gx", 0, 0, tiled=True)

    def unpack(*refs):
        unpack_kernel(width, *refs)

    return pl.pallas_call(
        unpack,
        out_shape=(
            jax.ShapeDtypeStruct(temp0.shape, jnp.float32),
            jax.ShapeDtypeStruct(kappa.shape, jnp.float32),
            jax.ShapeDtypeStruct(hface.shape, jnp.float32),
        ),
        in_specs=[vmem],
        out_specs=(vmem, vmem, vmem),
        compiler_params=params(2 * rows * cols + planes * OUT_ROWS * LANES),
    )(back)


def solution(mesh):
    placed = (
        P(("groups", "gx"), None, None),
        P(("groups", "gx"), None, None),
        P(("groups", "gx"), None, None),
        P(("groups", "gx"), None),
        P(("groups", "gx"), None),
        P("groups", None),
        P(("groups", "gx"), None, None),
    )
    return jax.shard_map(
        body,
        mesh=mesh,
        in_specs=placed,
        out_specs=(
            P(("groups", "gx"), None, None),
            P(("groups", "gx"), None, None),
            P(("groups", "gx"), None),
        ),
        check_vma=False,
    )
```

```python
import math

import jax
import jax.numpy as jnp
from jax import lax
from jax.experimental import pallas as pl
from jax.experimental.pallas import tpu as pltpu
from jax.sharding import PartitionSpec as P

LATENT = 1.5
MELT = 1.0
SPREAD = 0.15
DELTA = 0.05
EMISSION = 0.1
POWER = 8.0
AMBIENT = 0.2
SUBSTRATE = 0.5

LANES = 128
HALF = 64
LEFT = 96
UNROLL = 8
MIB = 1024 * 1024


def lane_iota(rows):
    return lax.broadcasted_iota(jnp.int32, (rows, LANES), 1)


ACT_LOW, ACT_HIGH, COT_RIGHT, COT_LEFT, FACE = 96, 50, 11, 75, 79


def in_rows(rows):
    return 2 * rows + rows // 2


def out_rows(rows):
    return rows + 1


def pack_kernel(parts, width, *refs):
    path, *sources = refs[:7]
    out, heat = refs[7:9]
    spots, temp, kappa, act, hface, codes, cot, faces, done = refs[9:]
    cols = temp.shape[-1]
    rows = temp.shape[1]
    half = rows // 2
    tiles = cols // LANES
    copies = [
        pltpu.make_async_copy(source, held, done.at[i])
        for i, (source, held) in enumerate(zip([path] + sources, (spots, temp, kappa, act, hface, codes, cot)))
    ]
    for copy in copies:
        copy.start()

    planes = heat.shape[1]
    base = lax.axis_index("gx") * width
    place = (lane_iota(planes) - lax.rem(base, LANES)) & (LANES - 1)
    col = base + jnp.where(place < LEFT, place, place - LANES)
    cell = lax.broadcasted_iota(jnp.int32, (planes, LANES), 0) * cols + col
    cell = jnp.where((col >= 0) & (col < cols), cell, -1)
    copies[0].wait()
    for n in range(heat.shape[0]):
        count = jnp.zeros((planes, LANES), jnp.float32)
        for s in range(spots.shape[1]):
            count = count + jnp.where(cell == spots[n, s], 1.0, 0.0)
        heat[n] = POWER * count

    for copy in copies[1:]:
        copy.wait()
    faces[0:8] = jnp.broadcast_to(hface[...], (8, cols))
    faces[8:16] = jnp.broadcast_to(codes[...].astype(jnp.float32), (8, cols))

    lane_of = lane_iota(rows)
    for d in range(parts):
        tile, off = divmod(d * width, LANES)
        lane = (lane_of - off) & (LANES - 1)

        def window(ref):
            def part(t):
                place = slice(min(max(t, 0), tiles - 1) * LANES, (min(max(t, 0), tiles - 1) + 1) * LANES)
                value = ref[0, :, place] if len(ref.shape) == 3 else ref[:, place]
                return value.astype(jnp.float32)

            count = ref.shape[-2]
            result = part(tile)
            if off > LANES - HALF - 7:
                result = jnp.where((lane_of[:count] < off) & (lane[:count] < LEFT), part(tile + 1), result)
            if off < 7:
                result = jnp.where((lane_of[:count] >= off) & (lane[:count] >= LEFT), part(tile - 1), result)
            return result

        t = window(temp)
        k = window(kappa)
        a = window(act)
        c = window(cot)
        face = window(faces)
        extra = jnp.where(
            lane >= 89,
            pltpu.roll(a, ACT_LOW, axis=1),
            jnp.where(lane >= 75, pltpu.roll(c, COT_RIGHT, axis=1), pltpu.roll(c, COT_LEFT, axis=1)),
        )
        face = jnp.concatenate(
            [pltpu.roll(x, FACE + 7 - 70, axis=1, stride=10, stride_axis=0) for x in (face[0:8], face[8:16])], axis=0
        )
        face = jnp.where((lane[:16] >= FACE) & (lane[:16] < 89), face, extra[:16])
        extra = jnp.concatenate([face, extra[16:]], axis=0)
        out[d, 0:rows] = jnp.where((lane >= 71) & (lane < 121), extra, t)
        out[d, rows : 2 * rows] = jnp.where((lane >= 75) & (lane < 121), pltpu.roll(a, ACT_HIGH, axis=1), k)
        out[d, 2 * rows : 2 * rows + half] = jnp.where(
            lane[:half] < HALF, c[:half], pltpu.roll(c[half:], HALF, axis=1)
        )


def reciprocal(value):
    return 1.0 / value


def shares(first, second):
    total = first + second
    positive = total > 0
    inverse = reciprocal(jnp.where(positive, total, 1.0))
    return first * inverse, second * inverse, positive


def window_kernel(
    cols, width, got, heat, out, temps, keffs, rates, gains, kap, acts, lam, mu, kgrad, hcoef, hgrad, hrow, crow, *faces
):
    steps, planes = heat.shape[:2]
    rows = temps.shape[2]
    half = rows // 2
    base = lax.axis_index("gx") * width
    lane = (lane_iota(rows) - lax.rem(base, LANES)) & (LANES - 1)
    depth = lax.broadcasted_iota(jnp.int32, (rows, LANES), 0)
    inner = depth < rows - 1
    top_row = lax.broadcasted_iota(jnp.int32, (8, LANES), 0) == 0
    column = base + jnp.where(lane < LEFT, lane, lane - LANES)
    inside = (column >= 0) & (column < cols)

    place = jnp.where(lane[:8] < LEFT, lane[:8], lane[:8] - LANES) + 7 - 10 * (7 - depth[:8])
    face_mask = (place >= 0) & (place < 10)

    def active(act, n):
        return jnp.where(act <= n, 1.0, 0.1)

    def unpack(p, carry):
        a = got[p, 0:rows]
        b = got[p, rows : 2 * rows]
        c = got[p, 2 * rows : 2 * rows + half]
        temps[0, p] = a
        k = jnp.where(inside, b, 0.0)
        kap[p] = k
        act = jnp.where(
            (lane < 25) | (lane >= 121),
            pltpu.roll(a, LANES - ACT_LOW, axis=1),
            pltpu.roll(b, LANES - ACT_HIGH, axis=1),
        )
        acts[p] = act
        cot = jnp.concatenate([c, pltpu.roll(c, HALF, axis=1)], axis=0)
        cot = jnp.where(
            lane < HALF,
            cot,
            jnp.where(lane < LEFT, pltpu.roll(a, LANES - COT_RIGHT, axis=1), pltpu.roll(a, LANES - COT_LEFT, axis=1)),
        )
        lam[p] = cot
        face = pltpu.roll(a[0:16], 112, axis=1)
        for bit in (1, 2, 4):
            face = jnp.where((depth[:16] & bit) > 0, pltpu.roll(face, LANES - 10 * bit, axis=1), face)
        hrow[pl.ds(p, 1)] = jnp.sum(jnp.where(face_mask, face[0:8], 0.0), axis=0, keepdims=True)
        crow[pl.ds(p, 1)] = jnp.sum(jnp.where(face_mask, face[8:16], 0.0), axis=0, keepdims=True)
        keffs[0, p] = k * active(act, 0.0) * (1.0 + 0.5 * a)
        return carry

    lax.fori_loop(0, planes, unpack, 0, unroll=UNROLL)
    zero = jnp.zeros((rows, LANES), jnp.float32)
    for n in range(steps):
        temps[n, planes] = zero
        keffs[n, planes] = zero
    mu[planes] = zero

    def forward(n):
        def step(p, behind):
            t = temps[n, p]
            a = keffs[n, p]

            def flow(axis, b, dt):
                first, second, positive = shares(a, b)
                half_g = a * second
                if faces:
                    faces[0][n, axis, p] = half_g
                    faces[0][n, axis + 1, p] = second * jnp.where(positive, second, 1.0) * dt
                    faces[0][n, axis + 2, p] = first * jnp.where(positive, first, 1.0) * dt
                return half_g * dt

            fx = flow(0, keffs[n, p + 1], temps[n, p + 1] - t)
            fy = flow(3, pltpu.roll(a, LANES - 1, axis=1), pltpu.roll(t, LANES - 1, axis=1) - t)
            fz = flow(6, pltpu.roll(a, rows - 1, axis=0), jnp.where(inner, pltpu.roll(t, rows - 1, axis=0) - t, 0.0))
            flux = 2.0 * ((fx - behind) + (fy - pltpu.roll(fy, 1, axis=1)) + (fz - pltpu.roll(fz, 1, axis=0)))
            shifted = t - MELT
            bump = LATENT * jnp.exp2(jnp.square(shifted) * (-1.0 / (SPREAD * SPREAD * math.log(2.0))))
            inv_c = reciprocal(1.0 + bump)
            rate = DELTA * inv_c
            t8 = t[0:8]
            h = hrow[pl.ds(p, 1)]
            code = crow[pl.ds(p, 1)]
            square = t8 * t8
            radiative = code == 1.0
            linear = t8 - jnp.where(code == 0.0, AMBIENT, SUBSTRATE)
            shape = jnp.where(radiative, EMISSION * (square * square - AMBIENT**4), linear)
            slope = jnp.where(radiative, 4.0 * EMISSION * square * t8, 1.0)
            surface = jnp.where(top_row, heat[n, pl.ds(p, 1)] - h * shape, 0.0)
            flux = jnp.concatenate([flux[0:8] + surface, flux[8:]], axis=0)
            dt = flux * rate
            gain = 1.0 + dt * (bump * inv_c) * (shifted * (2.0 / (SPREAD * SPREAD)))
            gain = jnp.concatenate([gain[0:8] - jnp.where(top_row, rate[0:8] * h * slope, 0.0), gain[8:]], axis=0)
            gains[n, p] = gain
            hcoef[n, pl.ds(p, 1)] = -(rate[0:8] * shape)[0:1]
            if n < steps - 1:
                rates[n, p] = rate
                after = t + dt
                temps[n + 1, p] = after
                keffs[n + 1, p] = kap[p] * active(acts[p], float(n + 1)) * (1.0 + 0.5 * after)
            else:
                mu[p] = lam[p] * rate
            return fx

        lax.fori_loop(0, planes, step, zero, unroll=UNROLL)

    for n in range(steps):
        forward(n)

    def backward(n):
        def step(p, carry, store=None):
            behind_e, behind_p = carry
            t = temps[n, p]
            m = mu[p]

            def adjoint(axis, dm, ends):
                if faces:
                    half_g, first, second = (faces[0][n, axis + i, p] for i in range(3))
                    return half_g * dm, first * dm, second * dm
                a = keffs[n, p]
                b, dt = ends(a)
                first, second, positive = shares(a, b)
                q = dt * dm
                return (
                    a * second * dm,
                    second * jnp.where(positive, second, 1.0) * q,
                    first * jnp.where(positive, first, 1.0) * q,
                )

            def rolled(axis, count):
                return lambda a: (pltpu.roll(a, count - 1, axis=axis), pltpu.roll(t, count - 1, axis=axis) - t)

            ex, px, qx = adjoint(0, mu[p + 1] - m, lambda a: (keffs[n, p + 1], temps[n, p + 1] - t))
            ey, py, qy = adjoint(3, pltpu.roll(m, LANES - 1, axis=1) - m, rolled(1, LANES))
            ez, pz, qz = adjoint(6, jnp.where(inner, pltpu.roll(m, rows - 1, axis=0) - m, 0.0), rolled(0, rows))
            energy = (ex - behind_e) + (ey - pltpu.roll(ey, 1, axis=1)) + (ez - pltpu.roll(ez, 1, axis=0))
            pull = (px + behind_p) + (py + pltpu.roll(qy, 1, axis=1)) + (pz + pltpu.roll(qz, 1, axis=0))
            on = active(acts[p], float(n))
            old = lam[p]
            new = old * gains[n, p] + 2.0 * energy - pull * (kap[p] * on)
            grad = pull * (on * (2.0 + t))
            hg = old[0:1] * hcoef[n, pl.ds(p, 1)]
            if n < steps - 1:
                grad = kgrad[p] + grad
                hg = hgrad[pl.ds(p, 1)] + hg
            if n > 0:
                lam[p] = new
                mu[p] = new * rates[n - 1, p]
                kgrad[p] = grad
                hgrad[pl.ds(p, 1)] = hg
            else:
                store(jnp.where(lane < HALF, new, pltpu.roll(-grad, HALF, axis=1)), hg)
            return ex, qx

        def last(i, carry):
            size = UNROLL * out_rows(rows)
            chunk = out.at[pl.ds(pl.multiple_of(i * size, 8), size)]
            for j in range(UNROLL):

                def store(cube, row, at=j * out_rows(rows)):
                    chunk[at : at + rows] = cube
                    chunk[at + rows : at + rows + 1] = row

                carry = step(i * UNROLL + j, carry, store)
            return carry

        if n > 0:
            lax.fori_loop(0, planes, step, (zero, zero), unroll=UNROLL)
        else:
            lax.fori_loop(0, planes // UNROLL, last, (zero, zero))

    for n in reversed(range(steps)):
        backward(n)


def unpack_kernel(width, got, adjoint, kgrad, hgrad):
    rows = adjoint.shape[1]
    per_tile = LANES // width
    lane = lane_iota(rows)
    turned = (lane - HALF) & (LANES - 1)
    for tile in range(adjoint.shape[2] // LANES):
        adj = grad = face = None
        for i in range(per_tile):
            at = (tile * per_tile + i) * out_rows(rows)
            part = got[at : at + rows]
            row = got[at + rows : at + rows + 1]
            adj = part if i == 0 else jnp.where(lane < i * width, adj, part)
            grad = part if i == 0 else jnp.where(turned < i * width, grad, part)
            face = row if i == 0 else jnp.where(lane[0:1] < i * width, face, row)
        place = slice(tile * LANES, (tile + 1) * LANES)
        adjoint[0, :, place] = adj
        kgrad[0, :, place] = pltpu.roll(grad, HALF, axis=1)
        hgrad[:, place] = face


def body(temp0, kappa, act_step, hface, codes, path, cotangent):
    parts = lax.axis_size("gx")
    cols = temp0.shape[2]
    rows = temp0.shape[1]
    width = cols // parts
    planes = parts * temp0.shape[0]
    steps = path.shape[0]
    vmem = pl.BlockSpec(memory_space=pltpu.VMEM)
    hbm = pl.BlockSpec(memory_space=pltpu.HBM)
    plane = rows * LANES

    def params(words):
        return pltpu.CompilerParams(vmem_limit_bytes=4 * words + 2 * MIB)

    def pack(*refs):
        pack_kernel(parts, width, *refs)

    sources = (temp0, kappa, act_step, hface, codes, cotangent)
    packed, heat = pl.pallas_call(
        pack,
        out_shape=(
            jax.ShapeDtypeStruct((parts, in_rows(rows), LANES), jnp.float32),
            jax.ShapeDtypeStruct((steps, planes, LANES), jnp.float32),
        ),
        in_specs=[hbm] * 7,
        out_specs=(vmem, vmem),
        scratch_shapes=[pltpu.SMEM(path.shape, path.dtype)]
        + [pltpu.VMEM(x.shape, x.dtype) for x in sources]
        + [pltpu.VMEM((16, cols), jnp.float32), pltpu.SemaphoreType.DMA((7,))],
        compiler_params=params(5 * rows * cols + parts * (in_rows(rows) + steps) * LANES),
    )(*[pltpu.with_memory_space_constraint(x, pltpu.HBM) for x in (path,) + sources])
    got = lax.all_to_all(packed, "gx", 0, 0, tiled=True)

    def compute(*refs):
        window_kernel(cols, width, *refs)

    keep = 9 * steps if planes <= 32 else 0

    def held(count, extra=0):
        return pltpu.VMEM(count + (planes + extra, rows, LANES), jnp.float32)

    row = pltpu.VMEM((planes, LANES), jnp.float32)
    result = pl.pallas_call(
        compute,
        out_shape=jax.ShapeDtypeStruct((planes * out_rows(rows), LANES), jnp.float32),
        in_specs=[vmem, vmem],
        out_specs=vmem,
        scratch_shapes=[
            held((steps,), 1),
            held((steps,), 1),
            held((steps - 1,)),
            held((steps,)),
            held(()),
            held(()),
            held(()),
            held((), 1),
            held(()),
            pltpu.VMEM((steps, planes, LANES), jnp.float32),
            row,
            row,
            row,
        ]
        + ([held((steps, 9))] if keep else []),
        compiler_params=params(planes * ((24 + keep) * plane + (in_rows(rows) + out_rows(rows)) * LANES)),
    )(got, heat)
    result = result.reshape(planes, out_rows(rows), 1, LANES)
    back = lax.all_to_all(result, "gx", 0, 0, tiled=True).reshape(planes * out_rows(rows), LANES)

    def unpack(*refs):
        unpack_kernel(width, *refs)

    return pl.pallas_call(
        unpack,
        out_shape=(
            jax.ShapeDtypeStruct(temp0.shape, jnp.float32),
            jax.ShapeDtypeStruct(kappa.shape, jnp.float32),
            jax.ShapeDtypeStruct(hface.shape, jnp.float32),
        ),
        in_specs=[vmem],
        out_specs=(vmem, vmem, vmem),
        compiler_params=params(2 * rows * cols + planes * out_rows(rows) * LANES),
    )(back)


def solution(mesh):
    placed = (
        P(("groups", "gx"), None, None),
        P(("groups", "gx"), None, None),
        P(("groups", "gx"), None, None),
        P(("groups", "gx"), None),
        P(("groups", "gx"), None),
        P("groups", None),
        P(("groups", "gx"), None, None),
    )
    return jax.shard_map(
        body,
        mesh=mesh,
        in_specs=placed,
        out_specs=(
            P(("groups", "gx"), None, None),
            P(("groups", "gx"), None, None),
            P(("groups", "gx"), None),
        ),
        check_vma=False,
    )
```

```python
import math

import jax
import jax.numpy as jnp
from jax import lax
from jax.experimental import pallas as pl
from jax.experimental.pallas import tpu as pltpu
from jax.sharding import PartitionSpec as P

LATENT = 1.5
MELT = 1.0
SPREAD = 0.15
DELTA = 0.05
EMISSION = 0.1
POWER = 8.0
AMBIENT = 0.2
SUBSTRATE = 0.5

LANES = 128
HALF = 64
LEFT = 96
UNROLL = 8
MIB = 1024 * 1024


def lane_iota(rows):
    return lax.broadcasted_iota(jnp.int32, (rows, LANES), 1)


ACT_LOW, ACT_HIGH, COT_RIGHT, COT_LEFT, FACE = 96, 50, 11, 75, 79


def in_rows(rows):
    return 2 * rows + rows // 2


def out_rows(rows):
    return rows + 1


def pack_kernel(parts, width, *refs):
    path, *sources = refs[:7]
    out, heat = refs[7:9]
    spots, temp, kappa, act, hface, codes, cot, faces, done = refs[9:]
    cols = temp.shape[-1]
    rows = temp.shape[1]
    half = rows // 2
    tiles = cols // LANES
    copies = [
        pltpu.make_async_copy(source, held, done.at[i])
        for i, (source, held) in enumerate(zip([path] + sources, (spots, temp, kappa, act, hface, codes, cot)))
    ]
    for copy in copies:
        copy.start()

    planes = heat.shape[1]
    base = lax.axis_index("gx") * width
    place = (lane_iota(planes) - lax.rem(base, LANES)) & (LANES - 1)
    col = base + jnp.where(place < LEFT, place, place - LANES)
    cell = lax.broadcasted_iota(jnp.int32, (planes, LANES), 0) * cols + col
    cell = jnp.where((col >= 0) & (col < cols), cell, -1)
    copies[0].wait()
    for n in range(heat.shape[0]):
        count = jnp.zeros((planes, LANES), jnp.float32)
        for s in range(spots.shape[1]):
            count = count + jnp.where(cell == spots[n, s], 1.0, 0.0)
        heat[n] = (0.5 * POWER) * count

    for copy in copies[1:]:
        copy.wait()
    faces[0:8] = jnp.broadcast_to(hface[...], (8, cols))
    faces[8:16] = jnp.broadcast_to(codes[...].astype(jnp.float32), (8, cols))

    lane_of = lane_iota(rows)
    for d in range(parts):
        tile, off = divmod(d * width, LANES)
        lane = (lane_of - off) & (LANES - 1)

        def window(ref):
            def part(t):
                place = slice(min(max(t, 0), tiles - 1) * LANES, (min(max(t, 0), tiles - 1) + 1) * LANES)
                value = ref[0, :, place] if len(ref.shape) == 3 else ref[:, place]
                return value.astype(jnp.float32)

            count = ref.shape[-2]
            result = part(tile)
            if off > LANES - HALF - 7:
                result = jnp.where((lane_of[:count] < off) & (lane[:count] < LEFT), part(tile + 1), result)
            if off < 7:
                result = jnp.where((lane_of[:count] >= off) & (lane[:count] >= LEFT), part(tile - 1), result)
            return result

        t = window(temp)
        k = window(kappa)
        a = window(act)
        c = window(cot)
        face = window(faces)
        extra = jnp.where(
            lane >= 89,
            pltpu.roll(a, ACT_LOW, axis=1),
            jnp.where(lane >= 75, pltpu.roll(c, COT_RIGHT, axis=1), pltpu.roll(c, COT_LEFT, axis=1)),
        )
        face = jnp.concatenate(
            [pltpu.roll(x, FACE + 7 - 70, axis=1, stride=10, stride_axis=0) for x in (face[0:8], face[8:16])], axis=0
        )
        face = jnp.where((lane[:16] >= FACE) & (lane[:16] < 89), face, extra[:16])
        extra = jnp.concatenate([face, extra[16:]], axis=0)
        out[d, 0:rows] = jnp.where((lane >= 71) & (lane < 121), extra, t)
        out[d, rows : 2 * rows] = jnp.where((lane >= 75) & (lane < 121), pltpu.roll(a, ACT_HIGH, axis=1), k)
        out[d, 2 * rows : 2 * rows + half] = jnp.where(
            lane[:half] < HALF, c[:half], pltpu.roll(c[half:], HALF, axis=1)
        )


def reciprocal(value):
    return 1.0 / value


def shares(first, second):
    total = first + second
    positive = total > 0
    inverse = reciprocal(jnp.where(positive, total, 1.0))
    return first * inverse, second * inverse, positive


def window_kernel(
    cols, width, got, heat, out, temps, keffs, rates, gains, kap, acts, lam, mu, kgrad, hcoef, hgrad, hrow, crow, *faces
):
    steps, planes = heat.shape[:2]
    rows = temps.shape[2]
    half = rows // 2
    base = lax.axis_index("gx") * width
    lane = (lane_iota(rows) - lax.rem(base, LANES)) & (LANES - 1)
    depth = lax.broadcasted_iota(jnp.int32, (rows, LANES), 0)
    bottom = lax.broadcasted_iota(jnp.int32, (8, LANES), 0) == 7
    top_row = lax.broadcasted_iota(jnp.int32, (8, LANES), 0) == 0
    column = base + jnp.where(lane < LEFT, lane, lane - LANES)
    inside = (column >= 0) & (column < cols)

    place = jnp.where(lane[:8] < LEFT, lane[:8], lane[:8] - LANES) + 7 - 10 * (7 - depth[:8])
    face_mask = (place >= 0) & (place < 10)

    def above_bottom(value):
        return jnp.concatenate([value[: rows - 8], jnp.where(bottom, 0.0, value[rows - 8 :])], axis=0)

    def active(act, n):
        return jnp.where(act <= n, 1.0, 0.1)

    def unpack(p, carry):
        a = got[p, 0:rows]
        b = got[p, rows : 2 * rows]
        c = got[p, 2 * rows : 2 * rows + half]
        temps[0, p] = a
        k = jnp.where(inside, b, 0.0)
        k = 0.5 * k
        kap[p] = k
        act = jnp.where(
            (lane < 25) | (lane >= 121),
            pltpu.roll(a, LANES - ACT_LOW, axis=1),
            pltpu.roll(b, LANES - ACT_HIGH, axis=1),
        )
        acts[p] = act
        cot = jnp.concatenate([c, pltpu.roll(c, HALF, axis=1)], axis=0)
        cot = jnp.where(
            lane < HALF,
            cot,
            jnp.where(lane < LEFT, pltpu.roll(a, LANES - COT_RIGHT, axis=1), pltpu.roll(a, LANES - COT_LEFT, axis=1)),
        )
        lam[p] = cot
        face = pltpu.roll(a[0:16], 112, axis=1)
        for bit in (1, 2, 4):
            face = jnp.where((depth[:16] & bit) > 0, pltpu.roll(face, LANES - 10 * bit, axis=1), face)
        hrow[pl.ds(p, 1)] = 0.5 * jnp.sum(jnp.where(face_mask, face[0:8], 0.0), axis=0, keepdims=True)
        crow[pl.ds(p, 1)] = jnp.sum(jnp.where(face_mask, face[8:16], 0.0), axis=0, keepdims=True)
        keffs[0, p] = k * active(act, 0.0) * (2.0 + a)
        return carry

    lax.fori_loop(0, planes, unpack, 0, unroll=UNROLL)
    zero = jnp.zeros((rows, LANES), jnp.float32)
    for n in range(steps):
        temps[n, planes] = zero
        keffs[n, planes] = zero
    mu[planes] = zero

    def forward(n):
        def ahead(p):
            return temps[n, p], keffs[n, p]

        def step(p, carry):
            behind, t, a = carry
            t_ahead, a_ahead = ahead(p + 1)

            def flow(axis, b, dt):
                first, second, positive = shares(a, b)
                half_g = a * second
                if faces:
                    faces[0][n, axis, p] = half_g
                    faces[0][n, axis + 1, p] = second * jnp.where(positive, second, 1.0) * dt
                    faces[0][n, axis + 2, p] = first * jnp.where(positive, first, 1.0) * dt
                return half_g * dt

            fx = flow(0, a_ahead, t_ahead - t)
            fy = flow(3, pltpu.roll(a, LANES - 1, axis=1), pltpu.roll(t, LANES - 1, axis=1) - t)
            fz = flow(6, pltpu.roll(a, rows - 1, axis=0), above_bottom(pltpu.roll(t, rows - 1, axis=0) - t))
            flux = (fx - behind) + (fy - pltpu.roll(fy, 1, axis=1)) + (fz - pltpu.roll(fz, 1, axis=0))
            shifted = t - MELT
            bump = LATENT * jnp.exp2(jnp.square(shifted) * (-1.0 / (SPREAD * SPREAD * math.log(2.0))))
            inv_c = reciprocal(1.0 + bump)
            rate = (2.0 * DELTA) * inv_c
            t8 = t[0:8]
            h = hrow[pl.ds(p, 1)]
            code = crow[pl.ds(p, 1)]
            square = t8 * t8
            radiative = code == 1.0
            linear = t8 - jnp.where(code == 0.0, AMBIENT, SUBSTRATE)
            shape = jnp.where(radiative, EMISSION * (square * square - AMBIENT**4), linear)
            slope = jnp.where(radiative, 4.0 * EMISSION * square * t8, 1.0)
            surface = jnp.where(top_row, heat[n, pl.ds(p, 1)] - h * shape, 0.0)
            flux = jnp.concatenate([flux[0:8] + surface, flux[8:]], axis=0)
            dt = flux * rate
            gain = 1.0 + dt * (bump * inv_c) * (shifted * (2.0 / (SPREAD * SPREAD)))
            gain = jnp.concatenate([gain[0:8] - jnp.where(top_row, rate[0:8] * h * slope, 0.0), gain[8:]], axis=0)
            gains[n, p] = gain
            hcoef[n, pl.ds(p, 1)] = (rate[0:8] * shape)[0:1]
            if n < steps - 1:
                rates[n, p] = rate
                after = t + dt
                temps[n + 1, p] = after
                keffs[n + 1, p] = kap[p] * active(acts[p], float(n + 1)) * (2.0 + after)
            else:
                mu[p] = lam[p] * rate
            return fx, t_ahead, a_ahead

        lax.fori_loop(0, planes, step, (zero,) + ahead(0), unroll=UNROLL)

    for n in range(steps):
        forward(n)

    def backward(n):
        def step(p, carry, store=None):
            behind_e, behind_p, m = carry
            t = temps[n, p]
            m_ahead = mu[p + 1]

            def adjoint(axis, dm, ends):
                if faces:
                    half_g, first, second = (faces[0][n, axis + i, p] for i in range(3))
                    return half_g * dm, first * dm, second * dm
                a = keffs[n, p]
                b, dt = ends(a)
                first, second, positive = shares(a, b)
                q = dt * dm
                return (
                    a * second * dm,
                    second * jnp.where(positive, second, 1.0) * q,
                    first * jnp.where(positive, first, 1.0) * q,
                )

            def rolled(axis, count):
                return lambda a: (pltpu.roll(a, count - 1, axis=axis), pltpu.roll(t, count - 1, axis=axis) - t)

            ex, px, qx = adjoint(0, m_ahead - m, lambda a: (keffs[n, p + 1], temps[n, p + 1] - t))
            ey, py, qy = adjoint(3, pltpu.roll(m, LANES - 1, axis=1) - m, rolled(1, LANES))
            ez, pz, qz = adjoint(6, above_bottom(pltpu.roll(m, rows - 1, axis=0) - m), rolled(0, rows))
            energy = (ex - behind_e) + (ey - pltpu.roll(ey, 1, axis=1)) + (ez - pltpu.roll(ez, 1, axis=0))
            pull = (px + behind_p) + (py + pltpu.roll(qy, 1, axis=1)) + (pz + pltpu.roll(qz, 1, axis=0))
            pull = pull * active(acts[p], float(n))
            old = lam[p]
            new = old * gains[n, p] + energy - pull * kap[p]
            grad = pull * (2.0 + t)
            hg = old[0:1] * hcoef[n, pl.ds(p, 1)]
            if n < steps - 1:
                grad = kgrad[p] + grad
                hg = hgrad[pl.ds(p, 1)] + hg
            if n > 0:
                lam[p] = new
                mu[p] = new * rates[n - 1, p]
                kgrad[p] = grad
                hgrad[pl.ds(p, 1)] = hg
            else:
                store(jnp.where(lane < HALF, new, pltpu.roll(-0.5 * grad, HALF, axis=1)), -0.5 * hg)
            return ex, qx, m_ahead

        def last(i, carry):
            size = UNROLL * out_rows(rows)
            chunk = out.at[pl.ds(pl.multiple_of(i * size, 8), size)]
            for j in range(UNROLL):

                def store(cube, row, at=j * out_rows(rows)):
                    chunk[at : at + rows] = cube
                    chunk[at + rows : at + rows + 1] = row

                carry = step(i * UNROLL + j, carry, store)
            return carry

        if n > 0:
            lax.fori_loop(0, planes, step, (zero, zero, mu[0]), unroll=UNROLL)
        else:
            lax.fori_loop(0, planes // UNROLL, last, (zero, zero, mu[0]))

    for n in reversed(range(steps)):
        backward(n)


def unpack_kernel(width, got, adjoint, kgrad, hgrad):
    rows = adjoint.shape[1]
    per_tile = LANES // width
    lane = lane_iota(rows)
    turned = (lane - HALF) & (LANES - 1)
    for tile in range(adjoint.shape[2] // LANES):
        adj = grad = face = None
        for i in range(per_tile):
            at = (tile * per_tile + i) * out_rows(rows)
            part = got[at : at + rows]
            row = got[at + rows : at + rows + 1]
            adj = part if i == 0 else jnp.where(lane < i * width, adj, part)
            grad = part if i == 0 else jnp.where(turned < i * width, grad, part)
            face = row if i == 0 else jnp.where(lane[0:1] < i * width, face, row)
        place = slice(tile * LANES, (tile + 1) * LANES)
        adjoint[0, :, place] = adj
        kgrad[0, :, place] = pltpu.roll(grad, HALF, axis=1)
        hgrad[:, place] = face


def body(temp0, kappa, act_step, hface, codes, path, cotangent):
    parts = lax.axis_size("gx")
    cols = temp0.shape[2]
    rows = temp0.shape[1]
    width = cols // parts
    planes = parts * temp0.shape[0]
    steps = path.shape[0]
    vmem = pl.BlockSpec(memory_space=pltpu.VMEM)
    hbm = pl.BlockSpec(memory_space=pltpu.HBM)
    plane = rows * LANES

    def params(words):
        return pltpu.CompilerParams(vmem_limit_bytes=4 * words + 2 * MIB)

    def pack(*refs):
        pack_kernel(parts, width, *refs)

    sources = (temp0, kappa, act_step, hface, codes, cotangent)
    packed, heat = pl.pallas_call(
        pack,
        out_shape=(
            jax.ShapeDtypeStruct((parts, in_rows(rows), LANES), jnp.float32),
            jax.ShapeDtypeStruct((steps, planes, LANES), jnp.float32),
        ),
        in_specs=[hbm] * 7,
        out_specs=(vmem, vmem),
        scratch_shapes=[pltpu.SMEM(path.shape, path.dtype)]
        + [pltpu.VMEM(x.shape, x.dtype) for x in sources]
        + [pltpu.VMEM((16, cols), jnp.float32), pltpu.SemaphoreType.DMA((7,))],
        compiler_params=params(5 * rows * cols + parts * (in_rows(rows) + steps) * LANES),
    )(*[pltpu.with_memory_space_constraint(x, pltpu.HBM) for x in (path,) + sources])
    got = lax.all_to_all(packed, "gx", 0, 0, tiled=True)

    def compute(*refs):
        window_kernel(cols, width, *refs)

    keep = 9 * steps if planes <= 32 else 0

    def held(count, extra=0):
        return pltpu.VMEM(count + (planes + extra, rows, LANES), jnp.float32)

    row = pltpu.VMEM((planes, LANES), jnp.float32)
    result = pl.pallas_call(
        compute,
        out_shape=jax.ShapeDtypeStruct((planes * out_rows(rows), LANES), jnp.float32),
        in_specs=[vmem, vmem],
        out_specs=vmem,
        scratch_shapes=[
            held((steps,), 1),
            held((steps,), 1),
            held((steps - 1,)),
            held((steps,)),
            held(()),
            held(()),
            held(()),
            held((), 1),
            held(()),
            pltpu.VMEM((steps, planes, LANES), jnp.float32),
            row,
            row,
            row,
        ]
        + ([held((steps, 9))] if keep else []),
        compiler_params=params(planes * ((24 + keep) * plane + (in_rows(rows) + out_rows(rows)) * LANES)),
    )(got, heat)
    result = result.reshape(planes, out_rows(rows), 1, LANES)
    back = lax.all_to_all(result, "gx", 0, 0, tiled=True).reshape(planes * out_rows(rows), LANES)

    def unpack(*refs):
        unpack_kernel(width, *refs)

    return pl.pallas_call(
        unpack,
        out_shape=(
            jax.ShapeDtypeStruct(temp0.shape, jnp.float32),
            jax.ShapeDtypeStruct(kappa.shape, jnp.float32),
            jax.ShapeDtypeStruct(hface.shape, jnp.float32),
        ),
        in_specs=[vmem],
        out_specs=(vmem, vmem, vmem),
        compiler_params=params(2 * rows * cols + planes * out_rows(rows) * LANES),
    )(back)


def solution(mesh):
    placed = (
        P(("groups", "gx"), None, None),
        P(("groups", "gx"), None, None),
        P(("groups", "gx"), None, None),
        P(("groups", "gx"), None),
        P(("groups", "gx"), None),
        P("groups", None),
        P(("groups", "gx"), None, None),
    )
    return jax.shard_map(
        body,
        mesh=mesh,
        in_specs=placed,
        out_specs=(
            P(("groups", "gx"), None, None),
            P(("groups", "gx"), None, None),
            P(("groups", "gx"), None),
        ),
        check_vma=False,
    )
```

```python
import math

import jax
import jax.numpy as jnp
from jax import lax
from jax.experimental import pallas as pl
from jax.experimental.pallas import tpu as pltpu
from jax.sharding import PartitionSpec as P

LATENT = 1.5
MELT = 1.0
SPREAD = 0.15
DELTA = 0.05
EMISSION = 0.1
POWER = 8.0
AMBIENT = 0.2
SUBSTRATE = 0.5

LANES = 128
HALF = 64
LEFT = 96
UNROLL = 16
MIB = 1024 * 1024


def lane_iota(rows):
    return lax.broadcasted_iota(jnp.int32, (rows, LANES), 1)


ACT_LOW, ACT_HIGH, COT_RIGHT, COT_LEFT, FACE = 96, 50, 11, 75, 79


def in_rows(rows):
    return 2 * rows + rows // 2


def out_rows(rows):
    return rows + 1


def pack_kernel(parts, width, *refs):
    path, *sources = refs[:7]
    out, heat = refs[7:9]
    spots, temp, kappa, act, hface, codes, cot, faces, done = refs[9:]
    cols = temp.shape[-1]
    rows = temp.shape[1]
    half = rows // 2
    tiles = cols // LANES
    copies = [
        pltpu.make_async_copy(source, held, done.at[i])
        for i, (source, held) in enumerate(zip([path] + sources, (spots, temp, kappa, act, hface, codes, cot)))
    ]
    for copy in copies:
        copy.start()

    planes = heat.shape[1]
    base = lax.axis_index("gx") * width
    place = (lane_iota(planes) - lax.rem(base, LANES)) & (LANES - 1)
    col = base + jnp.where(place < LEFT, place, place - LANES)
    cell = lax.broadcasted_iota(jnp.int32, (planes, LANES), 0) * cols + col
    cell = jnp.where((col >= 0) & (col < cols), cell, -1)
    copies[0].wait()
    for n in range(heat.shape[0]):
        count = jnp.zeros((planes, LANES), jnp.float32)
        for s in range(spots.shape[1]):
            count = count + jnp.where(cell == spots[n, s], 1.0, 0.0)
        heat[n] = (0.5 * POWER) * count

    for copy in copies[1:]:
        copy.wait()
    faces[0:8] = jnp.broadcast_to(hface[...], (8, cols))
    faces[8:16] = jnp.broadcast_to(codes[...].astype(jnp.float32), (8, cols))

    lane_of = lane_iota(rows)
    for d in range(parts):
        tile, off = divmod(d * width, LANES)
        lane = (lane_of - off) & (LANES - 1)

        def window(ref):
            def part(t):
                place = slice(min(max(t, 0), tiles - 1) * LANES, (min(max(t, 0), tiles - 1) + 1) * LANES)
                value = ref[0, :, place] if len(ref.shape) == 3 else ref[:, place]
                return value.astype(jnp.float32)

            count = ref.shape[-2]
            result = part(tile)
            if off > LANES - HALF - 7:
                result = jnp.where((lane_of[:count] < off) & (lane[:count] < LEFT), part(tile + 1), result)
            if off < 7:
                result = jnp.where((lane_of[:count] >= off) & (lane[:count] >= LEFT), part(tile - 1), result)
            return result

        t = window(temp)
        k = window(kappa)
        a = window(act)
        c = window(cot)
        face = window(faces)
        extra = jnp.where(
            lane >= 89,
            pltpu.roll(a, ACT_LOW, axis=1),
            jnp.where(lane >= 75, pltpu.roll(c, COT_RIGHT, axis=1), pltpu.roll(c, COT_LEFT, axis=1)),
        )
        face = jnp.concatenate(
            [pltpu.roll(x, FACE + 7 - 70, axis=1, stride=10, stride_axis=0) for x in (face[0:8], face[8:16])], axis=0
        )
        face = jnp.where((lane[:16] >= FACE) & (lane[:16] < 89), face, extra[:16])
        extra = jnp.concatenate([face, extra[16:]], axis=0)
        out[d, 0:rows] = jnp.where((lane >= 71) & (lane < 121), extra, t)
        out[d, rows : 2 * rows] = jnp.where((lane >= 75) & (lane < 121), pltpu.roll(a, ACT_HIGH, axis=1), k)
        out[d, 2 * rows : 2 * rows + half] = jnp.where(
            lane[:half] < HALF, c[:half], pltpu.roll(c[half:], HALF, axis=1)
        )


def reciprocal(value):
    return 1.0 / value


def shares(first, second):
    total = first + second
    positive = total > 0
    inverse = reciprocal(jnp.where(positive, total, 1.0))
    return first * inverse, second * inverse, positive


def window_kernel(
    cols, width, got, heat, out, temps, keffs, rates, gains, kap, acts, lam, mu, kgrad, hcoef, hrow, crow, *faces
):
    steps, planes = heat.shape[:2]
    rows = kap.shape[0]
    half = rows // 2
    unroll = UNROLL if planes <= 32 else 2
    base = lax.axis_index("gx") * width
    lane = (lane_iota(planes) - lax.rem(base, LANES)) & (LANES - 1)
    end = lax.broadcasted_iota(jnp.int32, (8, LANES), 0) == 7
    column = base + jnp.where(lane < LEFT, lane, lane - LANES)
    inside = (column >= 0) & (column < cols)
    zero = jnp.zeros((planes, LANES), jnp.float32)

    def before_end(value):
        return jnp.concatenate([value[: planes - 8], jnp.where(end, 0.0, value[planes - 8 :])], axis=0)

    def active(act, n):
        return jnp.where(act <= n, 1.0, 0.1)

    def layer(row):
        return got[pl.ds(row, planes, stride=in_rows(rows))]

    def unpack(q, carry):
        c = layer(2 * rows + q)
        for z, own in ((q, c), (q + half, pltpu.roll(c, HALF, axis=1))):
            a = layer(z)
            b = layer(rows + z)
            temps[0, z] = a
            k = 0.5 * jnp.where(inside, b, 0.0)
            kap[z] = k
            act = jnp.where(
                (lane < 25) | (lane >= 121),
                pltpu.roll(a, LANES - ACT_LOW, axis=1),
                pltpu.roll(b, LANES - ACT_HIGH, axis=1),
            )
            acts[z] = act
            lam[z] = jnp.where(
                lane < HALF,
                own,
                jnp.where(
                    lane < LEFT, pltpu.roll(a, LANES - COT_RIGHT, axis=1), pltpu.roll(a, LANES - COT_LEFT, axis=1)
                ),
            )
            keffs[0, z] = k * active(act, 0.0) * (2.0 + a)
        return carry

    lax.fori_loop(0, half, unpack, 0, unroll=unroll)

    place = jnp.where(lane < LEFT, lane, lane - LANES) + 7
    for held, first in ((hrow, 0), (crow, 8)):
        value = zero
        for r in range(8):
            block = 10 * (7 - r)
            moved = pltpu.roll(layer(first + r), LANES - (FACE + 7 - 70 + 10 * r), axis=1)
            value = jnp.where((place >= block) & (place < block + 10), moved, value)
        held[...] = value
    for n in range(steps):
        temps[n, rows] = zero
        keffs[n, rows] = zero
    mu[rows] = zero

    def forward(n):
        top = temps[n, 0]
        h = 0.5 * hrow[...]
        square = top * top
        radiative = crow[...] == 1.0
        linear = top - jnp.where(crow[...] == 0.0, AMBIENT, SUBSTRATE)
        shape = jnp.where(radiative, EMISSION * (square * square - AMBIENT**4), linear)
        slope = jnp.where(radiative, 4.0 * EMISSION * square * top, 1.0)

        def step(z, carry):
            behind, t, a = carry
            t_ahead, a_ahead = temps[n, z + 1], keffs[n, z + 1]

            def flow(axis, b, dt):
                first, second, positive = shares(a, b)
                half_g = a * second
                if faces:
                    faces[0][n, axis, z] = half_g
                    faces[0][n, axis + 1, z] = second * jnp.where(positive, second, 1.0) * dt
                    faces[0][n, axis + 2, z] = first * jnp.where(positive, first, 1.0) * dt
                return half_g * dt

            fz = flow(0, a_ahead, t_ahead - t)
            fy = flow(3, pltpu.roll(a, LANES - 1, axis=1), pltpu.roll(t, LANES - 1, axis=1) - t)
            fx = flow(6, pltpu.roll(a, planes - 1, axis=0), before_end(pltpu.roll(t, planes - 1, axis=0) - t))
            flux = (fz - behind) + (fy - pltpu.roll(fy, 1, axis=1)) + (fx - pltpu.roll(fx, 1, axis=0))
            shifted = t - MELT
            bump = LATENT * jnp.exp2(jnp.square(shifted) * (-1.0 / (SPREAD * SPREAD * math.log(2.0))))
            inv_c = reciprocal(1.0 + bump)
            rate = (2.0 * DELTA) * inv_c
            dt = flux * rate
            gains[n, z] = 1.0 + dt * (bump * inv_c) * (shifted * (2.0 / (SPREAD * SPREAD)))
            rates[n, z] = rate
            if n < steps - 1:
                after = t + dt
                temps[n + 1, z] = after
                keffs[n + 1, z] = kap[z] * active(acts[z], float(n + 1)) * (2.0 + after)
            else:
                mu[z] = lam[z] * rate
            return fz, t_ahead, a_ahead

        lax.fori_loop(0, rows, step, (h * shape - heat[n], top, keffs[n, 0]), unroll=unroll)
        rate = rates[n, 0]
        gains[n, 0] = gains[n, 0] - rate * h * slope
        hcoef[n] = rate * shape

    for n in range(steps):
        forward(n)

    def backward(n):
        def step(z, carry):
            behind_e, behind_p, m = carry
            t = temps[n, z]
            m_ahead = mu[z + 1]

            def adjoint(axis, dm, ends):
                if faces:
                    half_g, first, second = (faces[0][n, axis + i, z] for i in range(3))
                    return half_g * dm, first * dm, second * dm
                a = keffs[n, z]
                b, dt = ends(a)
                first, second, positive = shares(a, b)
                q = dt * dm
                return (
                    a * second * dm,
                    second * jnp.where(positive, second, 1.0) * q,
                    first * jnp.where(positive, first, 1.0) * q,
                )

            def rolled(axis, count):
                return lambda a: (pltpu.roll(a, count - 1, axis=axis), pltpu.roll(t, count - 1, axis=axis) - t)

            ez, pz, qz = adjoint(0, m_ahead - m, lambda a: (keffs[n, z + 1], temps[n, z + 1] - t))
            ey, py, qy = adjoint(3, pltpu.roll(m, LANES - 1, axis=1) - m, rolled(1, LANES))
            ex, px, qx = adjoint(6, before_end(pltpu.roll(m, planes - 1, axis=0) - m), rolled(0, planes))
            energy = (ez - behind_e) + (ey - pltpu.roll(ey, 1, axis=1)) + (ex - pltpu.roll(ex, 1, axis=0))
            pull = (pz + behind_p) + (py + pltpu.roll(qy, 1, axis=1)) + (px + pltpu.roll(qx, 1, axis=0))
            pull = pull * active(acts[z], float(n))
            new = lam[z] * gains[n, z] + energy - pull * kap[z]
            grad = pull * (2.0 + t)
            if n < steps - 1:
                grad = kgrad[z] + grad
            if n > 0:
                lam[z] = new
                mu[z] = new * rates[n - 1, z]
                kgrad[z] = grad
            else:
                out[pl.ds(z, planes, stride=out_rows(rows))] = jnp.where(
                    lane < HALF, new, pltpu.roll(-0.5 * grad, HALF, axis=1)
                )
            return ez, qz, m_ahead

        lax.fori_loop(0, rows, step, (zero, zero, mu[0]), unroll=unroll)

    total = zero
    for n in reversed(range(steps)):
        total = total + lam[0] * hcoef[n]
        backward(n)
    out[pl.ds(rows, planes, stride=out_rows(rows))] = -0.5 * total


def unpack_kernel(width, got, adjoint, kgrad, hgrad):
    rows = adjoint.shape[1]
    per_tile = LANES // width
    lane = lane_iota(rows)
    turned = (lane - HALF) & (LANES - 1)
    for tile in range(adjoint.shape[2] // LANES):
        adj = grad = face = None
        for i in range(per_tile):
            at = (tile * per_tile + i) * out_rows(rows)
            part = got[at : at + rows]
            row = got[at + rows : at + rows + 1]
            adj = part if i == 0 else jnp.where(lane < i * width, adj, part)
            grad = part if i == 0 else jnp.where(turned < i * width, grad, part)
            face = row if i == 0 else jnp.where(lane[0:1] < i * width, face, row)
        place = slice(tile * LANES, (tile + 1) * LANES)
        adjoint[0, :, place] = adj
        kgrad[0, :, place] = pltpu.roll(grad, HALF, axis=1)
        hgrad[:, place] = face


def body(temp0, kappa, act_step, hface, codes, path, cotangent):
    parts = lax.axis_size("gx")
    cols = temp0.shape[2]
    rows = temp0.shape[1]
    width = cols // parts
    planes = parts * temp0.shape[0]
    steps = path.shape[0]
    vmem = pl.BlockSpec(memory_space=pltpu.VMEM)
    hbm = pl.BlockSpec(memory_space=pltpu.HBM)
    plane = rows * LANES

    def params(words):
        return pltpu.CompilerParams(vmem_limit_bytes=4 * words + 2 * MIB)

    def pack(*refs):
        pack_kernel(parts, width, *refs)

    sources = (temp0, kappa, act_step, hface, codes, cotangent)
    packed, heat = pl.pallas_call(
        pack,
        out_shape=(
            jax.ShapeDtypeStruct((parts, in_rows(rows), LANES), jnp.float32),
            jax.ShapeDtypeStruct((steps, planes, LANES), jnp.float32),
        ),
        in_specs=[hbm] * 7,
        out_specs=(vmem, vmem),
        scratch_shapes=[pltpu.SMEM(path.shape, path.dtype)]
        + [pltpu.VMEM(x.shape, x.dtype) for x in sources]
        + [pltpu.VMEM((16, cols), jnp.float32), pltpu.SemaphoreType.DMA((7,))],
        compiler_params=params(5 * rows * cols + parts * (in_rows(rows) + steps) * LANES),
    )(*[pltpu.with_memory_space_constraint(x, pltpu.HBM) for x in (path,) + sources])
    got = lax.all_to_all(packed, "gx", 0, 0, tiled=True)

    def compute(*refs):
        window_kernel(cols, width, *refs)

    keep = 9 * steps if planes <= 32 else 0

    def held(count, extra=0):
        return pltpu.VMEM(count + (rows + extra, planes, LANES), jnp.float32)

    row = pltpu.VMEM((planes, LANES), jnp.float32)
    result = pl.pallas_call(
        compute,
        out_shape=jax.ShapeDtypeStruct((planes * out_rows(rows), LANES), jnp.float32),
        in_specs=[vmem, vmem],
        out_specs=vmem,
        scratch_shapes=[
            held((steps,), 1),
            held((steps,), 1),
            held((steps,)),
            held((steps,)),
            held(()),
            held(()),
            held(()),
            held((), 1),
            held(()),
            pltpu.VMEM((steps, planes, LANES), jnp.float32),
            row,
            row,
        ]
        + ([held((steps, 9))] if keep else []),
        compiler_params=params(planes * ((24 + keep) * plane + (in_rows(rows) + out_rows(rows)) * LANES)),
    )(got.reshape(planes * in_rows(rows), LANES), heat)
    result = result.reshape(planes, out_rows(rows), 1, LANES)
    back = lax.all_to_all(result, "gx", 0, 0, tiled=True).reshape(planes * out_rows(rows), LANES)

    def unpack(*refs):
        unpack_kernel(width, *refs)

    return pl.pallas_call(
        unpack,
        out_shape=(
            jax.ShapeDtypeStruct(temp0.shape, jnp.float32),
            jax.ShapeDtypeStruct(kappa.shape, jnp.float32),
            jax.ShapeDtypeStruct(hface.shape, jnp.float32),
        ),
        in_specs=[vmem],
        out_specs=(vmem, vmem, vmem),
        compiler_params=params(2 * rows * cols + planes * out_rows(rows) * LANES),
    )(back)


def solution(mesh):
    placed = (
        P(("groups", "gx"), None, None),
        P(("groups", "gx"), None, None),
        P(("groups", "gx"), None, None),
        P(("groups", "gx"), None),
        P(("groups", "gx"), None),
        P("groups", None),
        P(("groups", "gx"), None, None),
    )
    return jax.shard_map(
        body,
        mesh=mesh,
        in_specs=placed,
        out_specs=(
            P(("groups", "gx"), None, None),
            P(("groups", "gx"), None, None),
            P(("groups", "gx"), None),
        ),
        check_vma=False,
    )
```

```python
import math

import jax
import jax.numpy as jnp
from jax import lax
from jax.experimental import pallas as pl
from jax.experimental.pallas import tpu as pltpu
from jax.sharding import PartitionSpec as P

LATENT = 1.5
MELT = 1.0
SPREAD = 0.15
DELTA = 0.05
EMISSION = 0.1
POWER = 8.0
AMBIENT = 0.2
SUBSTRATE = 0.5

LANES = 128
HALF = 64
LEFT = 96
UNROLL = 16
MIB = 1024 * 1024


def lane_iota(rows):
    return lax.broadcasted_iota(jnp.int32, (rows, LANES), 1)


ACT_LOW, ACT_HIGH, COT_RIGHT, COT_LEFT = 96, 50, 11, 75


def in_rows(rows):
    return 2 * rows + rows // 2 + 2


def out_rows(rows):
    return rows + 1


def pack_kernel(parts, width, *refs):
    path, *sources = refs[:7]
    out, heat = refs[7:9]
    spots, temp, kappa, act, hface, codes, cot, done = refs[9:]
    cols = temp.shape[-1]
    rows = temp.shape[1]
    half = rows // 2
    tiles = cols // LANES
    copies = [
        pltpu.make_async_copy(source, held, done.at[i])
        for i, (source, held) in enumerate(zip([path] + sources, (spots, temp, kappa, act, hface, codes, cot)))
    ]
    for copy in copies:
        copy.start()

    planes = heat.shape[1]
    base = lax.axis_index("gx") * width
    place = (lane_iota(planes) - lax.rem(base, LANES)) & (LANES - 1)
    col = base + jnp.where(place < LEFT, place, place - LANES)
    cell = lax.broadcasted_iota(jnp.int32, (planes, LANES), 0) * cols + col
    cell = jnp.where((col >= 0) & (col < cols), cell, -1)
    copies[0].wait()
    for n in range(heat.shape[0]):
        count = jnp.zeros((planes, LANES), jnp.float32)
        for s in range(spots.shape[1]):
            count = count + jnp.where(cell == spots[n, s], 1.0, 0.0)
        heat[n] = (0.5 * POWER) * count

    for copy in copies[1:]:
        copy.wait()
    lane_of = lane_iota(rows)
    for d in range(parts):
        tile, off = divmod(d * width, LANES)
        lane = (lane_of - off) & (LANES - 1)

        def window(ref):
            def part(t):
                place = slice(min(max(t, 0), tiles - 1) * LANES, (min(max(t, 0), tiles - 1) + 1) * LANES)
                value = ref[0, :, place] if len(ref.shape) == 3 else ref[:, place]
                return value.astype(jnp.float32)

            count = ref.shape[-2]
            result = part(tile)
            if off > LANES - HALF - 7:
                result = jnp.where((lane_of[:count] < off) & (lane[:count] < LEFT), part(tile + 1), result)
            if off < 7:
                result = jnp.where((lane_of[:count] >= off) & (lane[:count] >= LEFT), part(tile - 1), result)
            return result

        t = window(temp)
        k = window(kappa)
        a = window(act)
        c = window(cot)
        extra = jnp.where(
            lane >= 89,
            pltpu.roll(a, ACT_LOW, axis=1),
            jnp.where(lane >= 75, pltpu.roll(c, COT_RIGHT, axis=1), pltpu.roll(c, COT_LEFT, axis=1)),
        )
        at = d * in_rows(rows)
        out[at : at + rows] = jnp.where((lane >= 71) & (lane < 121), extra, t)
        out[at + rows : at + 2 * rows] = jnp.where((lane >= 75) & (lane < 121), pltpu.roll(a, ACT_HIGH, axis=1), k)
        out[at + 2 * rows : at + 2 * rows + half] = jnp.where(
            lane[:half] < HALF, c[:half], pltpu.roll(c[half:], HALF, axis=1)
        )
        out[at + 2 * rows + half : at + 2 * rows + half + 1] = window(hface)
        out[at + 2 * rows + half + 1 : at + 2 * rows + half + 2] = window(codes)


def reciprocal(value):
    return 1.0 / value


def shares(first, second):
    total = first + second
    positive = total > 0
    inverse = reciprocal(jnp.where(positive, total, 1.0))
    return first * inverse, second * inverse, positive


def window_kernel(
    cols, width, got, heat, out, temps, keffs, rates, gains, kap, acts, lam, mu, kgrad, hcoef, hrow, crow, *faces
):
    steps, planes = heat.shape[:2]
    rows = kap.shape[0]
    half = rows // 2
    unroll = UNROLL if planes <= 32 else 2
    base = lax.axis_index("gx") * width
    lane = (lane_iota(planes) - lax.rem(base, LANES)) & (LANES - 1)
    end = lax.broadcasted_iota(jnp.int32, (8, LANES), 0) == 7
    column = base + jnp.where(lane < LEFT, lane, lane - LANES)
    inside = (column >= 0) & (column < cols)
    zero = jnp.zeros((planes, LANES), jnp.float32)

    def before_end(value):
        return jnp.concatenate([value[: planes - 8], jnp.where(end, 0.0, value[planes - 8 :])], axis=0)

    def active(act, n):
        return jnp.where(act <= n, 1.0, 0.1)

    def layer(row):
        return got[pl.ds(row, planes, stride=in_rows(rows))]

    def unpack(q, carry):
        c = layer(2 * rows + q)
        for z, own in ((q, c), (q + half, pltpu.roll(c, HALF, axis=1))):
            a = layer(z)
            b = layer(rows + z)
            temps[0, z] = a
            k = 0.5 * jnp.where(inside, b, 0.0)
            kap[z] = k
            act = jnp.where(
                (lane < 25) | (lane >= 121),
                pltpu.roll(a, LANES - ACT_LOW, axis=1),
                pltpu.roll(b, LANES - ACT_HIGH, axis=1),
            )
            acts[z] = act
            lam[z] = jnp.where(
                lane < HALF,
                own,
                jnp.where(
                    lane < LEFT, pltpu.roll(a, LANES - COT_RIGHT, axis=1), pltpu.roll(a, LANES - COT_LEFT, axis=1)
                ),
            )
            keffs[0, z] = k * active(act, 0.0) * (2.0 + a)
        return carry

    lax.fori_loop(0, half, unpack, 0, unroll=unroll)

    hrow[...] = layer(2 * rows + half)
    crow[...] = layer(2 * rows + half + 1)
    for n in range(steps):
        temps[n, rows] = zero
        keffs[n, rows] = zero
    mu[rows] = zero

    def forward(n):
        top = temps[n, 0]
        h = 0.5 * hrow[...]
        square = top * top
        radiative = crow[...] == 1.0
        linear = top - jnp.where(crow[...] == 0.0, AMBIENT, SUBSTRATE)
        shape = jnp.where(radiative, EMISSION * (square * square - AMBIENT**4), linear)
        slope = jnp.where(radiative, 4.0 * EMISSION * square * top, 1.0)

        def step(z, carry):
            behind, t, a = carry
            t_ahead, a_ahead = temps[n, z + 1], keffs[n, z + 1]

            def flow(axis, b, dt):
                first, second, positive = shares(a, b)
                half_g = a * second
                if faces:
                    faces[0][n, axis, z] = half_g
                    faces[0][n, axis + 1, z] = second * jnp.where(positive, second, 1.0) * dt
                    faces[0][n, axis + 2, z] = first * jnp.where(positive, first, 1.0) * dt
                return half_g * dt

            fz = flow(0, a_ahead, t_ahead - t)
            fy = flow(3, pltpu.roll(a, LANES - 1, axis=1), pltpu.roll(t, LANES - 1, axis=1) - t)
            fx = flow(6, pltpu.roll(a, planes - 1, axis=0), before_end(pltpu.roll(t, planes - 1, axis=0) - t))
            flux = (fz - behind) + (fy - pltpu.roll(fy, 1, axis=1)) + (fx - pltpu.roll(fx, 1, axis=0))
            shifted = t - MELT
            bump = (0.5 * LATENT / DELTA) * jnp.exp2(jnp.square(shifted) * (-1.0 / (SPREAD * SPREAD * math.log(2.0))))
            rate = reciprocal(0.5 / DELTA + bump)
            dt = flux * rate
            gains[n, z] = 1.0 + dt * (bump * rate) * (shifted * (2.0 / (SPREAD * SPREAD)))
            rates[n, z] = rate
            if n < steps - 1:
                after = t + dt
                temps[n + 1, z] = after
                keffs[n + 1, z] = kap[z] * active(acts[z], float(n + 1)) * (2.0 + after)
            else:
                mu[z] = lam[z] * rate
            return fz, t_ahead, a_ahead

        lax.fori_loop(0, rows, step, (h * shape - heat[n], top, keffs[n, 0]), unroll=unroll)
        rate = rates[n, 0]
        gains[n, 0] = gains[n, 0] - rate * h * slope
        hcoef[n] = rate * shape

    for n in range(steps):
        forward(n)

    def backward(n):
        def step(z, carry):
            behind_e, behind_p, m = carry
            t = temps[n, z]
            m_ahead = mu[z + 1]

            def adjoint(axis, dm, ends):
                if faces:
                    half_g, first, second = (faces[0][n, axis + i, z] for i in range(3))
                    return half_g * dm, first * dm, second * dm
                a = keffs[n, z]
                b, dt = ends(a)
                first, second, positive = shares(a, b)
                q = dt * dm
                return (
                    a * second * dm,
                    second * jnp.where(positive, second, 1.0) * q,
                    first * jnp.where(positive, first, 1.0) * q,
                )

            def rolled(axis, count):
                return lambda a: (pltpu.roll(a, count - 1, axis=axis), pltpu.roll(t, count - 1, axis=axis) - t)

            ez, pz, qz = adjoint(0, m_ahead - m, lambda a: (keffs[n, z + 1], temps[n, z + 1] - t))
            ey, py, qy = adjoint(3, pltpu.roll(m, LANES - 1, axis=1) - m, rolled(1, LANES))
            ex, px, qx = adjoint(6, before_end(pltpu.roll(m, planes - 1, axis=0) - m), rolled(0, planes))
            energy = (ez - behind_e) + (ey - pltpu.roll(ey, 1, axis=1)) + (ex - pltpu.roll(ex, 1, axis=0))
            pull = (pz + behind_p) + (py + pltpu.roll(qy, 1, axis=1)) + (px + pltpu.roll(qx, 1, axis=0))
            pull = pull * active(acts[z], float(n))
            new = lam[z] * gains[n, z] + energy - pull * kap[z]
            grad = pull * (2.0 + t)
            if n < steps - 1:
                grad = kgrad[z] + grad
            if n > 0:
                lam[z] = new
                mu[z] = new * rates[n - 1, z]
                kgrad[z] = grad
            else:
                out[pl.ds(z, planes, stride=out_rows(rows))] = jnp.where(
                    lane < HALF, new, pltpu.roll(-0.5 * grad, HALF, axis=1)
                )
            return ez, qz, m_ahead

        lax.fori_loop(0, rows, step, (zero, zero, mu[0]), unroll=unroll)

    total = zero
    for n in reversed(range(steps)):
        total = total + lam[0] * hcoef[n]
        backward(n)
    out[pl.ds(rows, planes, stride=out_rows(rows))] = -0.5 * total


def unpack_kernel(width, got, adjoint, kgrad, hgrad):
    rows = adjoint.shape[1]
    per_tile = LANES // width
    lane = lane_iota(rows)
    turned = (lane - HALF) & (LANES - 1)
    for tile in range(adjoint.shape[2] // LANES):
        adj = grad = face = None
        for i in range(per_tile):
            at = (tile * per_tile + i) * out_rows(rows)
            part = got[at : at + rows]
            row = got[at + rows : at + rows + 1]
            adj = part if i == 0 else jnp.where(lane < i * width, adj, part)
            grad = part if i == 0 else jnp.where(turned < i * width, grad, part)
            face = row if i == 0 else jnp.where(lane[0:1] < i * width, face, row)
        place = slice(tile * LANES, (tile + 1) * LANES)
        adjoint[0, :, place] = adj
        kgrad[0, :, place] = pltpu.roll(grad, HALF, axis=1)
        hgrad[:, place] = face


def body(temp0, kappa, act_step, hface, codes, path, cotangent):
    parts = lax.axis_size("gx")
    cols = temp0.shape[2]
    rows = temp0.shape[1]
    width = cols // parts
    planes = parts * temp0.shape[0]
    steps = path.shape[0]
    vmem = pl.BlockSpec(memory_space=pltpu.VMEM)
    hbm = pl.BlockSpec(memory_space=pltpu.HBM)
    plane = rows * LANES

    def params(words):
        return pltpu.CompilerParams(vmem_limit_bytes=4 * words + 2 * MIB)

    def pack(*refs):
        pack_kernel(parts, width, *refs)

    sources = (temp0, kappa, act_step, hface, codes, cotangent)
    packed, heat = pl.pallas_call(
        pack,
        out_shape=(
            jax.ShapeDtypeStruct((parts * in_rows(rows), LANES), jnp.float32),
            jax.ShapeDtypeStruct((steps, planes, LANES), jnp.float32),
        ),
        in_specs=[hbm] * 7,
        out_specs=(vmem, vmem),
        scratch_shapes=[pltpu.SMEM(path.shape, path.dtype)]
        + [pltpu.VMEM(x.shape, x.dtype) for x in sources]
        + [pltpu.SemaphoreType.DMA((7,))],
        compiler_params=params(5 * rows * cols + parts * (in_rows(rows) + steps) * LANES),
    )(*[pltpu.with_memory_space_constraint(x, pltpu.HBM) for x in (path,) + sources])
    packed = packed.reshape(parts, in_rows(rows), 1, LANES)
    got = lax.all_to_all(packed, "gx", 0, 0, tiled=True)

    def compute(*refs):
        window_kernel(cols, width, *refs)

    keep = 9 * steps if planes <= 32 else 0

    def held(count, extra=0):
        return pltpu.VMEM(count + (rows + extra, planes, LANES), jnp.float32)

    row = pltpu.VMEM((planes, LANES), jnp.float32)
    result = pl.pallas_call(
        compute,
        out_shape=jax.ShapeDtypeStruct((planes * out_rows(rows), LANES), jnp.float32),
        in_specs=[vmem, vmem],
        out_specs=vmem,
        scratch_shapes=[
            held((steps,), 1),
            held((steps,), 1),
            held((steps,)),
            held((steps,)),
            held(()),
            held(()),
            held(()),
            held((), 1),
            held(()),
            pltpu.VMEM((steps, planes, LANES), jnp.float32),
            row,
            row,
        ]
        + ([held((steps, 9))] if keep else []),
        compiler_params=params(planes * ((24 + keep) * plane + (in_rows(rows) + out_rows(rows)) * LANES)),
    )(got.reshape(planes * in_rows(rows), LANES), heat)
    result = result.reshape(planes, out_rows(rows), 1, LANES)
    back = lax.all_to_all(result, "gx", 0, 0, tiled=True).reshape(planes * out_rows(rows), LANES)

    def unpack(*refs):
        unpack_kernel(width, *refs)

    return pl.pallas_call(
        unpack,
        out_shape=(
            jax.ShapeDtypeStruct(temp0.shape, jnp.float32),
            jax.ShapeDtypeStruct(kappa.shape, jnp.float32),
            jax.ShapeDtypeStruct(hface.shape, jnp.float32),
        ),
        in_specs=[vmem],
        out_specs=(vmem, vmem, vmem),
        compiler_params=params(2 * rows * cols + planes * out_rows(rows) * LANES),
    )(back)


def solution(mesh):
    placed = (
        P(("groups", "gx"), None, None),
        P(("groups", "gx"), None, None),
        P(("groups", "gx"), None, None),
        P(("groups", "gx"), None),
        P(("groups", "gx"), None),
        P("groups", None),
        P(("groups", "gx"), None, None),
    )
    return jax.shard_map(
        body,
        mesh=mesh,
        in_specs=placed,
        out_specs=(
            P(("groups", "gx"), None, None),
            P(("groups", "gx"), None, None),
            P(("groups", "gx"), None),
        ),
        check_vma=False,
    )
```
